128 devices in a mesh: top: 8 (over x, core), leaf: 16 (over y, z).
Axes of the slice: x: 4, y: 4, z: 4, core: 2. Of those that a mesh axis runs over, the one named last changes fastest.
Arguments:
- points: float32 [3, 1048576], P(None, ('top', 'leaf')), may hold values from 0 to 16, as said below
- charges: float32 [16, 1048576], P(None, ('top', 'leaf')), may hold values from -6 to 6
- near_list: int32 [27, 16384], P(None, ('top', 'leaf')), may hold values from -1 to 16383, as said below
- far_list: int32 [16, 16384], P(None, ('top', 'leaf')), may hold values from 0 to 16383, as said below
- leaf_basis: float32 [64, 1048576], P(None, ('top', 'leaf')), may hold values from -0.75 to 0.75
- transfer: float32 [64, 1048576], P(None, ('top', 'leaf')), may hold values from -0.25 to 0.25
- leaf_skeleton: float32 [3, 1048576], P(None, ('top', 'leaf')), may hold values from 0 to 16, as said below
- device_far: int32 [4, 128], P(None, ('top', 'leaf')), may hold values from 0 to 127, as said below
- branch_transfer: float32 [64, 8192], P(None, ('top', 'leaf')), may hold values from -1.5 to 1.5
- device_skeleton: float32 [3, 8192], replicated, may hold values from 0 to 16, as said below
- branch_skeleton: float32 [3, 512], replicated, may hold values from 0 to 16, as said below
Outputs:
- product: float32 [16, 1048576], P(None, ('top', 'leaf'))
The draws below stay inside these ranges and needn't reach their ends.
Inputs may be any that keep to these rules, and one draw needn't show every extreme that they name: `near_list`: leaf c (d = c // 128, m = c % 128) has the cell (4 (d // 16) + m // 32, 4 (d % 16) + m // 8 % 4, m % 8) of a grid of cubes of side 0.25; slot 0 of leaf c is c itself, the other used slots name different leaves whose cells touch c's cell (face, edge or corner), a subset of them, in no fixed order, and the unused slots after them hold -1. `far_list`: 16 different leaves whose cells do not touch c's cell, while their parents (blocks of 2 x 2 x 2 cells aligned to even cell indices) touch or equal c's parent. `device_far`: 4 different device clusters of d's branch, each with an index 2 or more away from d's. The points of each leaf lie in its cell. `leaf_skeleton`: the skeleton points of each leaf lie in its cell. `device_skeleton`: the skeleton points of device cluster d lie in the box of its leaves' cells. `branch_skeleton`: the skeleton points of branch b lie in the box of its leaves' cells.
All inputs are finite; a program needn't handle non-finite values.
Results may differ from the reference program's by a relative error of at most 0.0003.
Values sent between devices are 32-bit elements; how exact they have to be, the bound alone decides.
No kernel may reach another device: no remote copies, remote signals or barrier semaphores. Data moves between devices by JAX's collectives and lax.ppermute only.
A program may use at most 128 MiB of HBM per device.

```python
import jax
import jax.numpy as jnp
from jax import lax

LEAF = 64
RANK = 64
RHS = 16
NEAR = 27
FAR = 16
DFAR = 4
BX = 4
BY = 4
BZ = 8
LEAVES_DEV = 128
GROUP = 16
BRANCHES = 8
DEVS = 128
LEAVES = 16384
POINTS = 1048576


CELL = 0.25


def leaf_cells():
    ident = jnp.arange(LEAVES, dtype=jnp.int32)
    device_id = ident // LEAVES_DEV
    local_id = ident % LEAVES_DEV
    first = BX * (device_id // GROUP) + local_id // (BY * BZ)
    second = BY * (device_id % GROUP) + local_id // BZ % BY
    third = local_id % BZ
    return jnp.stack([first, second, third])


def encode_cell(first, second, third):
    device_id = first // BX * GROUP + second // BY
    return device_id * LEAVES_DEV + (first % BX * BY + second % BY) * BZ + third


def inside_grid(first, second, third):
    return (first >= 0) & (first < BRANCHES * BX) & (second >= 0) & (second < GROUP * BY) & (third >= 0) & (third < BZ)


def fill_boxes(key, corners, extent, per_box, power):
    spread = jax.random.uniform(key, (3, corners.shape[1], per_box), jnp.float32) ** power
    sides = jnp.array(extent, jnp.float32)[:, None, None]
    placed = corners.astype(jnp.float32)[:, :, None] + spread * sides
    return (CELL * placed).reshape(3, -1)


def device_corners():
    device_id = jnp.arange(DEVS, dtype=jnp.int32)
    return jnp.stack([BX * (device_id // GROUP), BY * (device_id % GROUP), 0 * device_id])


def branch_corners():
    branch_id = jnp.arange(BRANCHES, dtype=jnp.int32)
    return jnp.stack([BX * branch_id, 0 * branch_id, 0 * branch_id])


def draw_points(key, part):
    key = jax.random.fold_in(key, 11)
    return fill_boxes(key, leaf_cells(), (1.0, 1.0, 1.0), LEAF, 1.0)


def draw_leaf_skeleton(key, part):
    key = jax.random.fold_in(key, 12)
    return fill_boxes(key, leaf_cells(), (1.0, 1.0, 1.0), RANK, 1.0)


def draw_device_skeleton(key, part):
    key = jax.random.fold_in(key, 13)
    return fill_boxes(key, device_corners(), (BX, BY, BZ), RANK, 1.0)


def draw_branch_skeleton(key, part):
    key = jax.random.fold_in(key, 14)
    return fill_boxes(key, branch_corners(), (BX, GROUP * BY, BZ), RANK, 1.0)


def draw_near_list(key, part):
    key = jax.random.fold_in(key, 21)
    cells = leaf_cells()
    offset_id = jnp.arange(27, dtype=jnp.int32)
    first = cells[0][:, None] + (offset_id // 9 - 1)[None, :]
    second = cells[1][:, None] + (offset_id // 3 % 3 - 1)[None, :]
    third = cells[2][:, None] + (offset_id % 3 - 1)[None, :]
    inside = inside_grid(first, second, third)
    neighbour = encode_cell(jnp.clip(first, 0, BRANCHES * BX - 1), jnp.clip(second, 0, GROUP * BY - 1), jnp.clip(third, 0, BZ - 1))
    jitter = jax.random.randint(key, (LEAVES, 27), 0, 4096)
    kept = (jitter < 3072) | (offset_id[None, :] == 13)
    scores = jitter * 32 + offset_id[None, :]
    scores = jnp.where(offset_id[None, :] == 13, 1 << 20, scores)
    scores = jnp.where(inside & kept, scores, -1)
    ranked, places = lax.top_k(scores, NEAR)
    chosen = jnp.take_along_axis(neighbour, places, axis=1)
    chosen = jnp.where(ranked >= 0, chosen, -1)
    return chosen.T.astype(jnp.int32)


def draw_far_list(key, part):
    key = jax.random.fold_in(key, 22)
    cells = leaf_cells()
    choice_id = jnp.arange(216, dtype=jnp.int32)
    first = 2 * (cells[0] // 2)[:, None] - 2 + (choice_id // 36)[None, :]
    second = 2 * (cells[1] // 2)[:, None] - 2 + (choice_id // 6 % 6)[None, :]
    third = 2 * (cells[2] // 2)[:, None] - 2 + (choice_id % 6)[None, :]
    apart = jnp.maximum(jnp.maximum(jnp.abs(first - cells[0][:, None]), jnp.abs(second - cells[1][:, None])), jnp.abs(third - cells[2][:, None]))
    usable = inside_grid(first, second, third) & (apart >= 2)
    neighbour = encode_cell(jnp.clip(first, 0, BRANCHES * BX - 1), jnp.clip(second, 0, GROUP * BY - 1), jnp.clip(third, 0, BZ - 1))
    jitter = jax.random.randint(key, (LEAVES, 216), 0, 4096)
    scores = jnp.where(usable, jitter * 256 + choice_id[None, :], -1)
    ranked, places = lax.top_k(scores, FAR)
    chosen = jnp.take_along_axis(neighbour, places, axis=1)
    return chosen.T.astype(jnp.int32)


def draw_device_far(key, part):
    key = jax.random.fold_in(key, 23)
    device_id = jnp.arange(DEVS, dtype=jnp.int32)
    member = device_id % GROUP
    column = jnp.arange(GROUP, dtype=jnp.int32)
    jitter = jax.random.randint(key, (DEVS, GROUP), 0, 4096)
    scores = jitter * GROUP + column[None, :]
    allowed = jnp.abs(column[None, :] - member[:, None]) >= 2
    scores = jnp.where(allowed, scores, -1)
    ranked, places = lax.top_k(scores, DFAR)
    chosen = ranked % GROUP + (device_id // GROUP * GROUP)[:, None]
    return chosen.T.astype(jnp.int32)


def shard_levels(rng, shape, shards, smallest, top_value):
    gain, own = 1.0, jax.random.fold_in(rng, 6)
    for position, blocks in shards:
        draws = jnp.exp(jax.random.uniform(jax.random.fold_in(own, position), (blocks,), jnp.float32, smallest / len(shards), top_value / len(shards)))
        gain = gain * jnp.repeat(draws, shape[position] // blocks).reshape([-1 if axis == position else 1 for axis in range(len(shape))])
    return gain


def scatter_about(own_key, shape, scale, reach, split=(), held_as=jnp.bfloat16):
    level = shard_levels(own_key, shape, split, -0.22, 0.18) if split else 1.0
    values = jax.random.normal(own_key, shape, jnp.float32) * scale * level
    return jnp.minimum(jnp.maximum(values, -reach), reach).astype(held_as)


def setup_inputs(seed: int = 0) -> dict:
    seeds = jax.random.split(jax.random.key(seed), 12)
    points = draw_points(jax.random.fold_in(seeds[11], 71), 0)
    charges = scatter_about(seeds[1], (RHS, POINTS), 1.0, 6.0, ((1, 128),), jnp.float32)
    near_list = draw_near_list(jax.random.fold_in(seeds[11], 71), 0)
    far_list = draw_far_list(jax.random.fold_in(seeds[11], 71), 0)
    leaf_basis = scatter_about(seeds[4], (RANK, POINTS), LEAF ** -0.5, 0.75, ((1, 128),), jnp.float32)
    transfer = scatter_about(seeds[5], (RANK, LEAVES * RANK), (max(RANK * LEAVES_DEV // 16, 1)) ** -0.5, 0.25, ((1, 128),), jnp.float32)
    leaf_skeleton = draw_leaf_skeleton(jax.random.fold_in(seeds[11], 71), 0)
    device_far = draw_device_far(jax.random.fold_in(seeds[11], 71), 0)
    branch_transfer = scatter_about(seeds[8], (RANK, DEVS * RANK), (max(RANK * GROUP // 64, 1)) ** -0.5, 1.5, ((1, 128),), jnp.float32)
    device_skeleton = draw_device_skeleton(jax.random.fold_in(seeds[11], 71), 0)
    branch_skeleton = draw_branch_skeleton(jax.random.fold_in(seeds[11], 71), 0)
    return {"points": points, "charges": charges, "near_list": near_list, "far_list": far_list, "leaf_basis": leaf_basis, "transfer": transfer, "leaf_skeleton": leaf_skeleton, "device_far": device_far, "branch_transfer": branch_transfer, "device_skeleton": device_skeleton, "branch_skeleton": branch_skeleton}


EXACT = lax.Precision.HIGHEST
KERNEL_SCALE = 3.4641016151377544
SIGNAL = 0.0625
NUGGET = 0.25

def kernel_tiles(targets, sources):
    differ = targets[..., :, None] - sources[..., None, :]
    distance = jnp.sqrt(lax.optimization_barrier(jnp.sum(differ * differ, axis=0)))
    scaled = KERNEL_SCALE * distance
    return SIGNAL * (1.0 + scaled) * jnp.exp(-scaled)

def near_block(target_pts, joined, leaf_ids):
    usable = (leaf_ids >= 0).astype(jnp.float32)
    source = jnp.take(joined, jnp.maximum(leaf_ids, 0), axis=1)
    entries = kernel_tiles(target_pts[:, None], source[:3])
    return jnp.einsum('sbij,sb,rsbj->rbi', entries, usable, source[3:], precision=EXACT)

def far_block(target_skel, joined, leaf_ids):
    source = jnp.take(joined, leaf_ids, axis=1)
    entries = kernel_tiles(target_skel[:, None], source[:3])
    return jnp.einsum('fbij,rfbj->rbi', entries, source[3:], precision=EXACT)

def reference(points, charges, near_list, far_list, leaf_basis, transfer, leaf_skeleton, device_far, branch_transfer, device_skeleton, branch_skeleton):
    coords = points.reshape(3, LEAVES, LEAF)
    values = charges.reshape(RHS, LEAVES, LEAF)
    joined = jnp.concatenate([coords, values], axis=0)
    basis_rows = leaf_basis.reshape(RANK, LEAVES, LEAF)
    coefficients = jnp.einsum('alk,rlk->rla', basis_rows, values, precision=EXACT)
    skeletons = leaf_skeleton.reshape(3, LEAVES, RANK)
    joined_coef = jnp.concatenate([skeletons, coefficients], axis=0)
    block_size = 64
    count_blocks = LEAVES // block_size

    def blocked(stacked):
        return jnp.moveaxis(stacked.reshape(stacked.shape[0], count_blocks, block_size, *stacked.shape[2:]), 1, 0)

    def near_step(inputs):
        return near_block(inputs[0], joined, inputs[1])

    def far_step(inputs):
        return far_block(inputs[0], joined_coef, inputs[1])
    near_out = lax.map(near_step, (blocked(coords), blocked(near_list)))
    near_out = jnp.moveaxis(near_out, 0, 1).reshape(RHS, LEAVES, LEAF)
    far_out = lax.map(far_step, (blocked(skeletons), blocked(far_list)))
    far_out = jnp.moveaxis(far_out, 0, 1).reshape(RHS, LEAVES, RANK)
    transfers = transfer.reshape(RANK, LEAVES, RANK)
    per_leaf = jnp.einsum('alb,rlb->lra', transfers, coefficients, precision=EXACT)
    device_coef = lax.optimization_barrier(jnp.sum(per_leaf.reshape(DEVS, LEAVES_DEV, RHS, RANK), axis=1))
    branch_tr = branch_transfer.reshape(RANK, DEVS, RANK)
    projected = jnp.einsum('adb,drb->dra', branch_tr, device_coef, precision=EXACT)
    branch_coef = lax.optimization_barrier(jnp.sum(projected.reshape(BRANCHES, GROUP, RHS, RANK), axis=1))
    device_skel = device_skeleton.reshape(3, DEVS, RANK)
    entries = kernel_tiles(device_skel[:, None], jnp.take(device_skel, device_far, axis=1))
    partner_coef = jnp.take(device_coef, device_far, axis=0)
    coupled = jnp.einsum('fdij,fdrj->dri', entries, partner_coef, precision=EXACT)
    branch_skel = branch_skeleton.reshape(3, BRANCHES, RANK)
    couplings = kernel_tiles(branch_skel[:, :, None, :], branch_skel[:, None, :, :])
    branch_order = jnp.arange(BRANCHES, dtype=jnp.int32)
    distant = (jnp.abs(branch_order[:, None] - branch_order[None, :]) >= 2).astype(jnp.float32)
    branch_field = jnp.einsum('bcij,bc,crj->bri', couplings, distant, branch_coef, precision=EXACT)
    coupled = coupled + jnp.einsum('adb,dra->drb', branch_tr, jnp.repeat(branch_field, GROUP, axis=0), precision=EXACT)
    leaf_field = far_out + jnp.einsum('alb,lra->rlb', transfers, jnp.repeat(coupled, LEAVES_DEV, axis=0), precision=EXACT)
    far_result = jnp.einsum('alk,rla->rlk', basis_rows, leaf_field, precision=EXACT)
    summed = near_out + far_result + NUGGET * values
    return summed.reshape(RHS, POINTS)
```

```python
import functools

import jax
import jax.numpy as jnp
from jax import lax
from jax.experimental import pallas as pl
from jax.experimental.pallas import tpu as pltpu
from jax.sharding import PartitionSpec as P

LEAF = 64
RHS = 16
BX = 4
BY = 4
BZ = 8
COLS = BX * BY
COL = BZ * LEAF
HERE = COLS * BZ
NEAR = 27
FAR = 16
NX = BX + 2
FX = BX + 4
NEAR_NULL = NX * NX * BZ
FAR_ALL = FX * FX * BZ
YFAR, YNEAR = 2 * BX, BX
XFAR, XNEAR = 2 * FX, NX
YCOLS = YFAR + YNEAR
XCOLS = XFAR + XNEAR
ROWS = RHS + 3
UNITS = 16

EXACT = lax.Precision.HIGHEST
KERNEL_SCALE = 3.4641016151377544
SIGNAL = 0.0625
NUGGET = 0.25
BF16 = jnp.bfloat16
F32 = jnp.float32
NT = (((1,), (1,)), ((), ()))
NN = (((1,), (0,)), ((), ()))
VMEM = pl.BlockSpec(memory_space=pltpu.VMEM)
SMEM = pl.BlockSpec(memory_space=pltpu.SMEM)
PARAMS = pltpu.CompilerParams(vmem_limit_bytes=50 * 2**20)


def dot(a, b, dims=NN):
    return lax.dot_general(a, b, dims, preferred_element_type=F32)


def halves(value):
    high = value.astype(BF16)
    return high, (value - high.astype(F32)).astype(BF16)


def low_lanes(rows):
    return lax.broadcasted_iota(jnp.int32, (rows, 128), 1) < LEAF


def column(index):
    return pl.ds(pl.multiple_of(index * COL, COL), COL)


def window_ids(ids, width, span, top, leaf, null):
    wx = ((ids >> 11) - top) * BX + ((ids >> 5) & 3) + width
    wy = (((ids >> 7) & 15) - leaf) * BY + ((ids >> 3) & 3) + width
    place = (wx * span + wy) * BZ + (ids & 7)
    place = jnp.minimum(jnp.maximum(place, 0), span * span * BZ - 1)
    return jnp.where(ids >= 0, place, null)


def first_kernel(
    points, charges, near_list, far_list, basis, transfer, skeleton, branch_transfer,
    coef, device_row, near_ids, far_ids, send_down, send_up,
):
    top, leaf = lax.axis_index("top"), lax.axis_index("leaf")
    listed = near_list[...]
    near_ids[0:NEAR] = window_ids(listed, 1, NX, top, leaf, NEAR_NULL)
    near_ids[NEAR : NEAR + 1] = jnp.full((1, HERE), NEAR_NULL, jnp.int32)
    near_ids[28:29] = jnp.sum((listed >= 0).astype(jnp.int32), axis=0, keepdims=True)
    far_ids[...] = window_ids(far_list[...], 2, FX, top, leaf, 0)

    lane = lax.broadcasted_iota(jnp.int32, (2 * RHS, 4 * LEAF), 1) // LEAF
    half = low_lanes(RHS)
    together = 4

    def coef_step(step, carry):
        places, products = [], []
        for part in range(together):
            place = pl.ds(pl.multiple_of((step * together + part) * 256, 256), 256)
            places.append(place)
            q_high, q_low = halves(charges[:, place])
            q = jnp.concatenate([q_high, q_low], axis=0)
            zero = jnp.zeros_like(q)
            rows = jnp.concatenate([jnp.where(lane == i, q, zero) for i in range(4)], axis=0)
            b_high, b_low = halves(basis[:, place])
            products.append(
                dot(rows, jnp.concatenate([b_high, b_high], axis=0), NT)
                + dot(rows, jnp.concatenate([b_low, b_low], axis=0), NT)
            )
        for place, product in zip(places, products):
            each = [product[32 * i : 32 * i + 16] + product[32 * i + 16 : 32 * i + 32] for i in range(4)]
            coef[:, place] = jnp.concatenate(
                [jnp.where(half, each[0], each[1]), jnp.where(half, each[2], each[3])], axis=1
            )
        return carry

    lax.fori_loop(0, HERE // 4 // together, coef_step, 0)

    def device_step(step, total):
        for part in range(together):
            place = pl.ds(pl.multiple_of((step * together + part) * 256, 256), 256)
            c = jnp.concatenate(halves(coef[:, place]), axis=0)
            t_high, t_low = halves(transfer[:, place])
            total = total + (dot(c, t_high, NT) + dot(c, t_low, NT))
        return total

    total = lax.fori_loop(0, HERE // 4 // together, device_step, jnp.zeros((2 * RHS, LEAF), F32))
    own = total[:RHS] + total[RHS:]
    raised = lax.dot_general(own, branch_transfer[...], NT, precision=EXACT, preferred_element_type=F32)
    device_row[...] = jnp.concatenate([own, raised], axis=1)

    def fill(target, near_y, far_y):
        for x in range(BX):
            for y in range(2):
                to, at = column(x * 2 + y), column(x * BY + far_y + y)
                target[0:RHS, to] = coef[:, at]
                target[RHS:ROWS, to] = skeleton[:, at]
            to, at = column(YFAR + x), column(x * BY + near_y)
            target[0:RHS, to] = charges[:, at]
            target[RHS:ROWS, to] = points[:, at]

    fill(send_down, 0, 0)
    fill(send_up, BY - 1, BY - 2)


def side_kernel(points, charges, skeleton, coef, from_down, from_up, send_left, send_right):
    def fill(target, near_x, far_x):
        for x in range(2):
            at_x = far_x + x
            for y in range(2):
                target[:, column(x * FX + y)] = from_down[:, column(at_x * 2 + y)]
                target[:, column(x * FX + y + BY + 2)] = from_up[:, column(at_x * 2 + y)]
            to = pl.ds((x * FX + 2) * COL, BY * COL)
            at = pl.ds(at_x * BY * COL, BY * COL)
            target[0:RHS, to] = coef[:, at]
            target[RHS:ROWS, to] = skeleton[:, at]
        target[:, column(XFAR)] = from_down[:, column(YFAR + near_x)]
        target[:, column(XFAR + BY + 1)] = from_up[:, column(YFAR + near_x)]
        to = pl.ds((XFAR + 1) * COL, BY * COL)
        at = pl.ds(near_x * BY * COL, BY * COL)
        target[0:RHS, to] = charges[:, at]
        target[RHS:ROWS, to] = points[:, at]

    fill(send_left, 0, 0)
    fill(send_right, BX - 1, BX - 2)


def build_column(coords, values, centre, col, sources, charge, targets=None, leaf=None):
    place = (coords - centre) * KERNEL_SCALE
    high = place.astype(BF16).astype(F32)
    rest = place - high
    mid = rest.astype(BF16).astype(F32)
    low = rest - mid
    norm = jnp.sum(place * place, axis=0, keepdims=True)
    norm_high = norm.astype(BF16).astype(F32)
    norm_rest = norm - norm_high
    norm_mid = norm_rest.astype(BF16).astype(F32)
    norm_low = norm_rest - norm_mid
    one = jnp.ones_like(norm)
    empty = jnp.zeros((8, COL), F32)
    rows = jnp.concatenate(
        [high, high, norm_high, norm_mid, high, mid, norm_low, one, mid, low, one, one, empty], axis=0
    )
    half = low_lanes(32)
    half_values = low_lanes(RHS)
    scaled = values * SIGNAL
    for pair in range(BZ // 2):
        lanes = slice(pair * 128, pair * 128 + 128)
        tile, tile_values = rows[:, lanes], scaled[:, lanes]
        turned, turned_values = pltpu.roll(tile, LEAF, 1), pltpu.roll(tile_values, LEAF, 1)
        at = col * BZ + 2 * pair
        sources[at] = jnp.where(half, tile, turned).astype(BF16)
        sources[at + 1] = jnp.where(half, turned, tile).astype(BF16)
        charge[at] = jnp.concatenate(halves(jnp.where(half_values, tile_values, turned_values)), axis=0)
        charge[at + 1] = jnp.concatenate(halves(jnp.where(half_values, turned_values, tile_values)), axis=0)
    if targets is not None:
        rows = jnp.concatenate(
            [
                -2.0 * high, -2.0 * mid, one, one, -2.0 * low, -2.0 * high, one, norm_high,
                -2.0 * mid, -2.0 * high, norm_mid, norm_low, empty,
            ],
            axis=0,
        )
        for pair in range(BZ // 2):
            tile = rows[:, pair * 128 : pair * 128 + 128].T.astype(BF16)
            targets[leaf + 2 * pair] = tile[:LEAF]
            targets[leaf + 2 * pair + 1] = tile[LEAF:]


def main_kernel(
    near_ids, far_ids, points, charges, skeleton, coef, from_down, from_up, from_left, from_right,
    near_out, far_out,
    near_sources, near_charge, near_targets, far_sources, far_charge, far_targets, squares, entries, sums, counts,
):
    top, leaf = lax.axis_index("top"), lax.axis_index("leaf")
    row = lax.broadcasted_iota(jnp.int32, (3, COL), 0)
    centre = jnp.where(
        row == 0, top.astype(F32) + 0.5, jnp.where(row == 1, leaf.astype(F32) + 0.5, 1.0)
    )

    def region(array, first, count, to, sources, charge):
        def step(i, carry):
            at = column(first + i)
            build_column(array[RHS:ROWS, at], array[0:RHS, at], centre, to(i), sources, charge)
            return carry

        lax.fori_loop(0, count, step, 0)

    def own(coords, values, to, sources, charge, targets):
        def step(i, carry):
            at = column(i)
            build_column(coords[:, at], values[:, at], centre, to(i), sources, charge, targets, i * BZ)
            return carry

        lax.fori_loop(0, COLS, step, 0)

    own(points, charges, lambda i: (i // BY + 1) * NX + i % BY + 1, near_sources, near_charge, near_targets)
    region(from_down, YFAR, YNEAR, lambda i: (i + 1) * NX, near_sources, near_charge)
    region(from_up, YFAR, YNEAR, lambda i: (i + 1) * NX + NX - 1, near_sources, near_charge)
    region(from_left, XFAR, XNEAR, lambda i: i, near_sources, near_charge)
    region(from_right, XFAR, XNEAR, lambda i: (NX - 1) * NX + i, near_sources, near_charge)
    near_sources[NEAR_NULL] = jnp.zeros((32, 128), BF16)
    near_charge[NEAR_NULL] = jnp.zeros((32, 128), BF16)
    own(skeleton, coef, lambda i: (i // BY + 2) * FX + i % BY + 2, far_sources, far_charge, far_targets)
    region(from_down, 0, YFAR, lambda i: (i // 2 + 2) * FX + i % 2, far_sources, far_charge)
    region(from_up, 0, YFAR, lambda i: (i // 2 + 2) * FX + i % 2 + BY + 2, far_sources, far_charge)
    region(from_left, 0, XFAR, lambda i: i, far_sources, far_charge)
    region(from_right, 0, XFAR, lambda i: (BX + 2) * FX + i, far_sources, far_charge)

    half = low_lanes(32)
    half_sums = low_lanes(RHS)

    def gathered(array, ids, slot, target):
        four = [array[ids[slot + k, target]] for k in range(4)]
        return jnp.concatenate([jnp.where(half, four[0], four[1]), jnp.where(half, four[2], four[3])], axis=1)

    def entries_of(unit):
        square = jnp.maximum(squares[unit], 1e-20)
        scaled = square * lax.rsqrt(square)
        high, low = halves((1.0 + scaled) * jnp.exp(-scaled))
        entries[unit, 0:LEAF] = high
        entries[unit, LEAF : 2 * LEAF] = low

    def clear():
        for unit in range(UNITS):
            squares[unit] = jnp.full((LEAF, 4 * LEAF), 1e6, F32)
            entries[unit] = jnp.zeros((2 * LEAF, 4 * LEAF), BF16)

    def near_leaf(group, unit):
        inner = unit * BZ + group + 1
        outer = ((group - 6) * (COLS // 2) + unit // 2) * BZ + (unit % 2) * (BZ - 1)
        return jnp.where(group < 6, inner, outer)

    for group in range(8):
        most = near_ids[28, near_leaf(group, 0)]
        for unit in range(1, UNITS):
            most = jnp.maximum(most, near_ids[28, near_leaf(group, unit)])
        counts[group] = jnp.minimum((most + 3) // 4, 7)

    def zero(i, carry):
        sums[i] = jnp.zeros((RHS, 128), F32)
        return carry

    lax.fori_loop(0, HERE, zero, 0)
    clear()
    steps = counts[0]
    for group in range(1, 8):
        steps = steps + counts[group]

    def near_step(step, state):
        (group, part), later, last = state
        for unit in range(UNITS):
            target = near_leaf(last[0], unit)
            product = dot(gathered(near_charge, near_ids, last[1] * 4, target), entries[unit], NT)
            sums[target] = sums[target] + (product[:RHS] + product[RHS:])
            entries_of(unit)
            target = near_leaf(group, unit)
            squares[unit] = dot(near_targets[target], gathered(near_sources, near_ids, part * 4, target))
        over = part + 1 >= counts[group]
        following = (
            jnp.where(over, jnp.minimum(group + 1, 7), group),
            jnp.where(over, 0, part + 1),
        )
        return following, (group, part), later

    start = (jnp.int32(0), jnp.int32(0))
    lax.fori_loop(0, steps + 2, near_step, (start, start, start))

    def near_store(i, carry):
        place = pl.ds(pl.multiple_of(i * 128, 128), 128)
        first, second = sums[2 * i], sums[2 * i + 1]
        first = first + pltpu.roll(first, LEAF, 1)
        second = second + pltpu.roll(second, LEAF, 1)
        near_out[:, place] = jnp.where(half_sums, first, second) + NUGGET * charges[:, place]
        return carry

    lax.fori_loop(0, HERE // 2, near_store, 0)

    clear()

    def far_step(step, carry):
        after = jnp.minimum(step, HERE // 4 - 1) * 4
        before = jnp.maximum(step - 2, 0) * 4
        for i in range(4):
            total = jnp.zeros((2 * RHS, 128), F32)
            for part in range(4):
                unit = i * 4 + part
                total = total + dot(gathered(far_charge, far_ids, part * 4, before + i), entries[unit], NT)
                entries_of(unit)
                squares[unit] = dot(
                    far_targets[after + i], gathered(far_sources, far_ids, part * 4, after + i)
                )
            sums[before + i] = total[:RHS] + total[RHS:]
        return carry

    lax.fori_loop(0, HERE // 4 + 2, far_step, 0)

    def far_store(i, carry):
        place = pl.ds(pl.multiple_of(i * 128, 128), 128)
        first, second = sums[2 * i], sums[2 * i + 1]
        first = first + pltpu.roll(first, LEAF, 1)
        second = second + pltpu.roll(second, LEAF, 1)
        far_out[:, place] = jnp.where(half_sums, first, second)
        return carry

    lax.fori_loop(0, HERE // 2, far_store, 0)


def last_kernel(
    device_far, rows, device_skeleton, branch_skeleton, branch_transfer, transfer, basis, near, far, out
):
    top, leaf = lax.axis_index("top"), lax.axis_index("leaf")
    same = lax.broadcasted_iota(jnp.int32, (LEAF, LEAF), 0) == lax.broadcasted_iota(
        jnp.int32, (LEAF, LEAF), 1
    )

    def upright(coords):
        return [
            jnp.sum(jnp.where(same, coords[i : i + 1], 0.0), axis=1, keepdims=True) for i in range(3)
        ]

    def block(own, other):
        total = 0.0
        for i in range(3):
            differ = own[i] - other[i : i + 1]
            total = total + differ * differ
        scaled = KERNEL_SCALE * jnp.sqrt(total)
        return SIGNAL * (1.0 + scaled) * jnp.exp(-scaled)

    def exact(a, b, dims):
        return lax.dot_general(a, b, dims, precision=EXACT, preferred_element_type=F32)

    own = upright(device_skeleton[top * 16 + leaf])
    coupled = jnp.zeros((RHS, LEAF), F32)
    for k in range(4):
        partner = jnp.minimum(jnp.maximum(device_far[k, 0], 0), 127)
        coupled = coupled + exact(rows[partner][:, :LEAF], block(own, device_skeleton[partner]), NT)
    own = upright(branch_skeleton[top])
    field = jnp.zeros((RHS, LEAF), F32)
    for e in range(8):
        total = rows[16 * e]
        for d in range(1, 16):
            total = total + rows[16 * e + d]
        weight = jnp.where(jnp.abs(e - top) >= 2, 1.0, 0.0)
        field = field + exact(total[:, LEAF:] * weight, block(own, branch_skeleton[e]), NT)
    coupled = coupled + exact(field, branch_transfer[...], NN)
    lifted = jnp.concatenate(halves(coupled), axis=0)
    half = low_lanes(RHS)
    together = 4

    def step(index, carry):
        places, fields = [], []
        for part in range(together):
            place = pl.ds(pl.multiple_of((index * together + part) * 256, 256), 256)
            t_high, t_low = halves(transfer[:, place])
            up = dot(lifted, t_high) + dot(lifted, t_low)
            places.append(place)
            fields.append(far[:, place] + (up[:RHS] + up[RHS:]))
        products = []
        for place, value in zip(places, fields):
            pieces = []
            for i in range(4):
                tile = value[:, (i // 2) * 128 : (i // 2) * 128 + 128]
                tile = jnp.where(half, tile, 0.0) if i % 2 == 0 else jnp.where(half, 0.0, tile)
                pieces.extend(halves(tile))
            lines = jnp.concatenate(pieces, axis=0)
            b_high, b_low = halves(basis[:, place])
            products.append(
                dot(lines, jnp.concatenate([b_high, b_high], axis=0))
                + dot(lines, jnp.concatenate([b_low, b_low], axis=0))
            )
        for place, product in zip(places, products):
            each = [product[32 * i : 32 * i + 16] + product[32 * i + 16 : 32 * i + 32] for i in range(4)]
            result = jnp.concatenate(
                [
                    jnp.where(half, each[0][:, :128], each[1][:, :128]),
                    jnp.where(half, each[2][:, 128:], each[3][:, 128:]),
                ],
                axis=1,
            )
            out[:, place] = near[:, place] + result
        return carry

    lax.fori_loop(0, HERE // 4 // together, step, 0)


def shape(*dims, dtype=F32):
    return jax.ShapeDtypeStruct(dims, dtype)


def body(
    points,
    charges,
    near_list,
    far_list,
    leaf_basis,
    transfer,
    leaf_skeleton,
    device_far,
    branch_transfer,
    device_skeleton,
    branch_skeleton,
):
    here = charges.shape[1]

    def moved(array, axis, up):
        size = lax.axis_size(axis)
        pairs = [(i, i + 1) for i in range(size - 1)]
        return lax.ppermute(array, axis, pairs if up else [(j, i) for i, j in pairs])

    coef, device_row, near_ids, far_ids, send_down, send_up = pl.pallas_call(
        first_kernel,
        in_specs=[VMEM] * 8,
        out_specs=[VMEM] * 6,
        out_shape=[
            shape(RHS, here), shape(RHS, 128), shape(32, HERE, dtype=jnp.int32), shape(FAR, HERE, dtype=jnp.int32),
            shape(ROWS, YCOLS * COL), shape(ROWS, YCOLS * COL),
        ],
        compiler_params=PARAMS,
        name="coefficients",
    )(points, charges, near_list, far_list, leaf_basis, transfer, leaf_skeleton, branch_transfer)
    every_row = lax.all_gather(device_row, ("top", "leaf"), axis=0)
    from_down = moved(send_up, "leaf", True)
    from_up = moved(send_down, "leaf", False)
    send_left, send_right = pl.pallas_call(
        side_kernel,
        in_specs=[VMEM] * 6,
        out_specs=[VMEM] * 2,
        out_shape=[shape(ROWS, XCOLS * COL), shape(ROWS, XCOLS * COL)],
        compiler_params=PARAMS,
        name="sides",
    )(points, charges, leaf_skeleton, coef, from_down, from_up)
    from_left = moved(send_right, "top", True)
    from_right = moved(send_left, "top", False)
    near, far = pl.pallas_call(
        main_kernel,
        in_specs=[SMEM] * 2 + [VMEM] * 8,
        out_specs=[VMEM] * 2,
        out_shape=[shape(RHS, here), shape(RHS, here)],
        scratch_shapes=[
            pltpu.VMEM((NEAR_NULL + 1, 32, 128), BF16),
            pltpu.VMEM((NEAR_NULL + 1, 32, 128), BF16),
            pltpu.VMEM((HERE, LEAF, 32), BF16),
            pltpu.VMEM((FAR_ALL, 32, 128), BF16),
            pltpu.VMEM((FAR_ALL, 32, 128), BF16),
            pltpu.VMEM((HERE, LEAF, 32), BF16),
            pltpu.VMEM((UNITS, LEAF, 4 * LEAF), F32),
            pltpu.VMEM((UNITS, 2 * LEAF, 4 * LEAF), BF16),
            pltpu.VMEM((HERE, RHS, 128), F32),
            pltpu.SMEM((8,), jnp.int32),
        ],
        compiler_params=PARAMS,
        cost_estimate=pl.CostEstimate(flops=10**11, bytes_accessed=10**7, transcendentals=4 * 10**7),
        name="lists",
    )(near_ids, far_ids, points, charges, leaf_skeleton, coef, from_down, from_up, from_left, from_right)
    return pl.pallas_call(
        last_kernel,
        in_specs=[SMEM] + [VMEM] * 8,
        out_specs=VMEM,
        out_shape=shape(RHS, here),
        compiler_params=PARAMS,
        name="fields",
    )(
        device_far,
        every_row,
        device_skeleton.reshape(3, -1, LEAF).transpose(1, 0, 2),
        branch_skeleton.reshape(3, -1, LEAF).transpose(1, 0, 2),
        branch_transfer,
        transfer,
        leaf_basis,
        near,
        far,
    )


def solution(mesh):
    split = P(None, ("top", "leaf"))
    return jax.shard_map(
        body, mesh=mesh, in_specs=(split,) * 9 + (P(), P()), out_specs=split, check_vma=False
    )
```

```python
import jax
import jax.numpy as jnp
from jax import lax
from jax.experimental import pallas as pl
from jax.experimental.pallas import tpu as pltpu
from jax.sharding import PartitionSpec as P

LEAF = 64
RHS = 16
BX = 4
BY = 4
BZ = 8
COLS = BX * BY
COL = BZ * LEAF
HERE = COLS * BZ
NEAR = 27
FAR = 16
NX = BX + 2
FX = BX + 4
NEAR_NULL = NX * NX * BZ
FAR_ALL = FX * FX * BZ
YFAR, YNEAR = 2 * BX, BX
XFAR, XNEAR = 2 * FX, NX
YCOLS = YFAR + YNEAR
XCOLS = XFAR + XNEAR
ROWS = RHS + 3
UNITS = 32
INNER = ((1, 1), (1, 2), (2, 1), (2, 2))
STRIP = ((1, 0), (1, 3), (2, 0), (2, 3))
RIM = tuple((x, y) for x in (0, 3) for y in range(4))

EXACT = lax.Precision.HIGHEST
KERNEL_SCALE = 3.4641016151377544
SIGNAL = 0.0625
NUGGET = 0.25
BF16 = jnp.bfloat16
F32 = jnp.float32
NT = (((1,), (1,)), ((), ()))
NN = (((1,), (0,)), ((), ()))
VMEM = pl.BlockSpec(memory_space=pltpu.VMEM)
SMEM = pl.BlockSpec(memory_space=pltpu.SMEM)
PARAMS = pltpu.CompilerParams(vmem_limit_bytes=60 * 2**20)


def dot(a, b, dims=NN):
    return lax.dot_general(a, b, dims, preferred_element_type=F32)


def halves(value):
    high = value.astype(BF16)
    return high, (value - high.astype(F32)).astype(BF16)


def low_lanes(rows):
    return lax.broadcasted_iota(jnp.int32, (rows, 128), 1) < LEAF


def column(index):
    return pl.ds(pl.multiple_of(index * COL, COL), COL)


def window_ids(ids, width, span, top, leaf, null):
    wx = ((ids >> 11) - top) * BX + ((ids >> 5) & 3) + width
    wy = (((ids >> 7) & 15) - leaf) * BY + ((ids >> 3) & 3) + width
    place = (wx * span + wy) * BZ + (ids & 7)
    place = jnp.minimum(jnp.maximum(place, 0), span * span * BZ - 1)
    return jnp.where(ids >= 0, place, null)


def work_lists(used, work):
    lane = lax.broadcasted_iota(jnp.int32, (1, HERE), 1)
    inner_x = (((lane >> 5) + 1) & 2) != 0
    inner_y = ((((lane >> 3) & 3) + 1) & 2) != 0
    member = jnp.where(inner_x, jnp.where(inner_y, 0, 1), 2)
    parts = (used + 3) >> 2
    first = lax.broadcasted_iota(jnp.int32, (HERE, HERE), 0)
    second = lax.broadcasted_iota(jnp.int32, (HERE, HERE), 1)
    place = lax.broadcasted_iota(jnp.int32, (HERE, 512), 1)
    for phase in range(3):
        kept = jnp.where(member == phase, parts, 0)
        end = jnp.sum(jnp.where(second <= first, kept, 0), axis=1, keepdims=True)
        count = jnp.sum(jnp.where(second == first, kept, 0), axis=1, keepdims=True)
        passed = end <= place
        leaf = jnp.sum(jnp.where(passed, 1, 0), axis=0, keepdims=True)
        start = jnp.sum(jnp.where(passed, count, 0), axis=0, keepdims=True)
        code = leaf * 8 + (place[:1] - start)
        work[phase : phase + 1] = jnp.where(leaf < HERE, code, 7)
        work[4 + phase : 5 + phase] = jnp.zeros((1, 512), jnp.int32) + jnp.sum(kept, axis=1, keepdims=True)


def first_kernel(
    points, charges, near_list, far_list, basis, transfer, skeleton, branch_transfer,
    coef, device_row, near_ids, far_ids, work, send_down, send_up,
):
    top, leaf = lax.axis_index("top"), lax.axis_index("leaf")
    listed = near_list[...]
    near_ids[0:NEAR] = window_ids(listed, 1, NX, top, leaf, NEAR_NULL)
    near_ids[NEAR:32] = jnp.full((5, HERE), NEAR_NULL, jnp.int32)
    work_lists(jnp.sum((listed >= 0).astype(jnp.int32), axis=0, keepdims=True), work)
    far_ids[...] = window_ids(far_list[...], 2, FX, top, leaf, 0)

    lane = lax.broadcasted_iota(jnp.int32, (2 * RHS, 4 * LEAF), 1) // LEAF
    half = low_lanes(RHS)
    together = 4

    def coef_step(step, carry):
        places, products = [], []
        for part in range(together):
            place = pl.ds(pl.multiple_of((step * together + part) * 256, 256), 256)
            places.append(place)
            q_high, q_low = halves(charges[:, place])
            q = jnp.concatenate([q_high, q_low], axis=0)
            zero = jnp.zeros_like(q)
            rows = jnp.concatenate([jnp.where(lane == i, q, zero) for i in range(4)], axis=0)
            b_high, b_low = halves(basis[:, place])
            products.append(
                dot(rows, jnp.concatenate([b_high, b_high], axis=0), NT)
                + dot(rows, jnp.concatenate([b_low, b_low], axis=0), NT)
            )
        for place, product in zip(places, products):
            each = [product[32 * i : 32 * i + 16] + product[32 * i + 16 : 32 * i + 32] for i in range(4)]
            coef[:, place] = jnp.concatenate(
                [jnp.where(half, each[0], each[1]), jnp.where(half, each[2], each[3])], axis=1
            )
        return carry

    lax.fori_loop(0, HERE // 4 // together, coef_step, 0)

    def device_step(step, total):
        for part in range(together):
            place = pl.ds(pl.multiple_of((step * together + part) * 256, 256), 256)
            c = jnp.concatenate(halves(coef[:, place]), axis=0)
            t_high, t_low = halves(transfer[:, place])
            total = total + (dot(c, t_high, NT) + dot(c, t_low, NT))
        return total

    total = lax.fori_loop(0, HERE // 4 // together, device_step, jnp.zeros((2 * RHS, LEAF), F32))
    own = total[:RHS] + total[RHS:]
    raised = lax.dot_general(own, branch_transfer[...], NT, precision=EXACT, preferred_element_type=F32)
    device_row[...] = jnp.concatenate([own, raised], axis=1)

    def fill(target, near_y, far_y):
        for x in range(BX):
            for y in range(2):
                to, at = column(x * 2 + y), column(x * BY + far_y + y)
                target[0:RHS, to] = coef[:, at]
                target[RHS:ROWS, to] = skeleton[:, at]
            to, at = column(YFAR + x), column(x * BY + near_y)
            target[0:RHS, to] = charges[:, at]
            target[RHS:ROWS, to] = points[:, at]

    fill(send_down, 0, 0)
    fill(send_up, BY - 1, BY - 2)


def side_kernel(points, charges, skeleton, coef, from_down, from_up, send_left, send_right):
    def fill(target, near_x, far_x):
        for x in range(2):
            at_x = far_x + x
            for y in range(2):
                target[:, column(x * FX + y)] = from_down[:, column(at_x * 2 + y)]
                target[:, column(x * FX + y + BY + 2)] = from_up[:, column(at_x * 2 + y)]
            to = pl.ds((x * FX + 2) * COL, BY * COL)
            at = pl.ds(at_x * BY * COL, BY * COL)
            target[0:RHS, to] = coef[:, at]
            target[RHS:ROWS, to] = skeleton[:, at]
        target[:, column(XFAR)] = from_down[:, column(YFAR + near_x)]
        target[:, column(XFAR + BY + 1)] = from_up[:, column(YFAR + near_x)]
        to = pl.ds((XFAR + 1) * COL, BY * COL)
        at = pl.ds(near_x * BY * COL, BY * COL)
        target[0:RHS, to] = charges[:, at]
        target[RHS:ROWS, to] = points[:, at]

    fill(send_left, 0, 0)
    fill(send_right, BX - 1, BX - 2)


def pieces_of(coords, centre):
    place = (coords - centre) * KERNEL_SCALE
    high = place.astype(BF16).astype(F32)
    rest = place - high
    mid = rest.astype(BF16).astype(F32)
    norm = jnp.sum(place * place, axis=0, keepdims=True)
    norm_high = norm.astype(BF16).astype(F32)
    norm_rest = norm - norm_high
    norm_mid = norm_rest.astype(BF16).astype(F32)
    return high, mid, rest - mid, norm_high, norm_mid, norm_rest - norm_mid


def build_column(coords, values, centre, col, sources, charge):
    high, mid, low, norm_high, norm_mid, norm_low = pieces_of(coords, centre)
    one = jnp.ones_like(norm_high)
    empty = jnp.zeros((8, COL), F32)
    rows = jnp.concatenate(
        [high, high, norm_high, norm_mid, high, mid, norm_low, one, mid, low, one, one, empty], axis=0
    )
    half = low_lanes(32)
    half_values = low_lanes(RHS)
    scaled = values * SIGNAL
    for pair in range(BZ // 2):
        lanes = slice(pair * 128, pair * 128 + 128)
        tile, tile_values = rows[:, lanes], scaled[:, lanes]
        turned, turned_values = pltpu.roll(tile, LEAF, 1), pltpu.roll(tile_values, LEAF, 1)
        at = col * BZ + 2 * pair
        sources[at] = jnp.where(half, tile, turned).astype(BF16)
        sources[at + 1] = jnp.where(half, turned, tile).astype(BF16)
        charge[at] = jnp.concatenate(halves(jnp.where(half_values, tile_values, turned_values)), axis=0)
        charge[at + 1] = jnp.concatenate(halves(jnp.where(half_values, turned_values, tile_values)), axis=0)


def build_targets(coords, centre, targets, leaf):
    high, mid, low, norm_high, norm_mid, norm_low = pieces_of(coords, centre)
    one = jnp.ones_like(norm_high)
    rows = jnp.concatenate(
        [
            -2.0 * high, -2.0 * mid, one, one, -2.0 * low, -2.0 * high, one, norm_high,
            -2.0 * mid, -2.0 * high, norm_mid, norm_low, jnp.zeros((8, COL), F32),
        ],
        axis=0,
    )
    for pair in range(BZ // 2):
        tile = rows[:, pair * 128 : pair * 128 + 128].T.astype(BF16)
        targets[leaf + 2 * pair] = tile[:LEAF]
        targets[leaf + 2 * pair + 1] = tile[LEAF:]


def centre_of():
    top, leaf = lax.axis_index("top"), lax.axis_index("leaf")
    row = lax.broadcasted_iota(jnp.int32, (3, COL), 0)
    return jnp.where(row == 0, top.astype(F32) + 0.5, jnp.where(row == 1, leaf.astype(F32) + 0.5, 1.0))


def region(array, first, count, to, centre, sources, charge):
    def step(i, carry):
        at = column(first + i)
        build_column(array[RHS:ROWS, at], array[0:RHS, at], centre, to(i), sources, charge)
        return carry

    lax.fori_loop(0, count, step, 0)


def own_columns(coords, values, to, centre, sources, charge):
    def step(i, carry):
        at = column(i)
        build_column(coords[:, at], values[:, at], centre, to(i), sources, charge)
        return carry

    lax.fori_loop(0, COLS, step, 0)


def gathered(array, ids, slot, target):
    half = low_lanes(32)
    four = [array[ids[slot + k, target]] for k in range(4)]
    return jnp.concatenate([jnp.where(half, four[0], four[1]), jnp.where(half, four[2], four[3])], axis=1)


def entries_of(square):
    square = jnp.maximum(square, 1e-20)
    scaled = square * lax.rsqrt(square)
    decay = jnp.exp(-scaled)
    return jnp.concatenate(halves(decay + scaled * decay), axis=0)


def list_steps(steps, choose, ids, sources, charge, targets, squares, add):
    def distances(step, unit):
        target, slot = choose(step, unit)
        squares[unit] = dot(targets[target], gathered(sources, ids, slot, target))

    for unit in range(UNITS):
        distances(0, unit)

    def run(step, carry):
        waiting = None
        for unit in range(UNITS + 1):
            if unit < UNITS:
                entries = entries_of(squares[unit])
                distances(jnp.minimum(step + 1, steps - 1), unit)
            if waiting is not None:
                target, slot = choose(step, unit - 1)
                product = dot(gathered(charge, ids, slot, target), waiting, NT)
                add(step, unit - 1, target, product[:RHS] + product[RHS:])
            waiting = entries
        return carry

    lax.fori_loop(0, steps, run, 0)


def near_pass(phase, cells, near_ids, work, points, centre, sources, charge, targets, squares, sums):
    for x, y in cells:
        col = x * BY + y
        build_targets(points[:, col * COL : col * COL + COL], centre, targets, col * BZ)

        def zero(i, carry, first=col * BZ):
            sums[first + i] = jnp.zeros((RHS, 128), F32)
            return carry

        lax.fori_loop(0, BZ, zero, 0)
    sources[NEAR_NULL] = jnp.zeros((32, 128), BF16)
    charge[NEAR_NULL] = jnp.zeros((32, 128), BF16)

    def choose(step, unit):
        code = work[phase, step * UNITS + unit]
        return code >> 3, (code & 7) * 4

    def add(step, unit, target, value):
        sums[target] = sums[target] + value

    steps = jnp.maximum((work[4 + phase, 0] + UNITS - 1) // UNITS, 1)
    list_steps(steps, choose, near_ids, sources, charge, targets, squares, add)


def folded(sums, pair):
    first, second = sums[2 * pair], sums[2 * pair + 1]
    first = first + pltpu.roll(first, LEAF, 1)
    second = second + pltpu.roll(second, LEAF, 1)
    return jnp.where(low_lanes(RHS), first, second)


def near_store(cells, out, places, sums, charges):
    for (x, y), to in zip(cells, places):
        for pair in range(BZ // 2):
            at = (x * BY + y) * COL + pair * 128
            value = folded(sums, (x * BY + y) * (BZ // 2) + pair)
            out[:, to * COL + pair * 128 : to * COL + pair * 128 + 128] = value + NUGGET * charges[:, at : at + 128]


def near_own(points, charges, centre, sources, charge):
    own_columns(points, charges, lambda i: (i // BY + 1) * NX + i % BY + 1, centre, sources, charge)


def near_sides(from_down, from_up, centre, sources, charge):
    region(from_down, YFAR, YNEAR, lambda i: (i + 1) * NX, centre, sources, charge)
    region(from_up, YFAR, YNEAR, lambda i: (i + 1) * NX + NX - 1, centre, sources, charge)


def inner_kernel(near_ids, work, points, charges, out, sources, charge, targets, squares, sums):
    centre = centre_of()
    near_own(points, charges, centre, sources, charge)
    near_pass(0, INNER, near_ids, work, points, centre, sources, charge, targets, squares, sums)
    near_store(INNER, out, range(4), sums, charges)


def strip_kernel(
    near_ids, work, points, charges, from_down, from_up, out, sources, charge, targets, squares, sums
):
    centre = centre_of()
    near_own(points, charges, centre, sources, charge)
    near_sides(from_down, from_up, centre, sources, charge)
    near_pass(1, STRIP, near_ids, work, points, centre, sources, charge, targets, squares, sums)
    near_store(STRIP, out, range(4), sums, charges)


def rest_kernel(
    near_ids, work, far_ids, points, charges, skeleton, coef, from_down, from_up, from_left, from_right,
    inner, strip, near_out, far_out,
    sources, charge, targets, far_sources, far_charge, far_targets, squares, sums,
):
    centre = centre_of()
    near_own(points, charges, centre, sources, charge)
    near_sides(from_down, from_up, centre, sources, charge)
    region(from_left, XFAR, XNEAR, lambda i: i, centre, sources, charge)
    region(from_right, XFAR, XNEAR, lambda i: (NX - 1) * NX + i, centre, sources, charge)
    near_pass(2, RIM, near_ids, work, points, centre, sources, charge, targets, squares, sums)
    near_store(RIM, near_out, [x * BY + y for x, y in RIM], sums, charges)
    for cells, done in ((INNER, inner), (STRIP, strip)):
        for i, (x, y) in enumerate(cells):
            near_out[:, column(x * BY + y)] = done[:, i * COL : i * COL + COL]

    own_columns(
        skeleton, coef, lambda i: (i // BY + 2) * FX + i % BY + 2, centre, far_sources, far_charge
    )

    def target_step(i, carry):
        build_targets(skeleton[:, column(i)], centre, far_targets, i * BZ)
        return carry

    lax.fori_loop(0, COLS, target_step, 0)
    region(from_down, 0, YFAR, lambda i: (i // 2 + 2) * FX + i % 2, centre, far_sources, far_charge)
    region(from_up, 0, YFAR, lambda i: (i // 2 + 2) * FX + i % 2 + BY + 2, centre, far_sources, far_charge)
    region(from_left, 0, XFAR, lambda i: i, centre, far_sources, far_charge)
    region(from_right, 0, XFAR, lambda i: (BX + 2) * FX + i, centre, far_sources, far_charge)

    def choose(step, unit):
        return step * (UNITS // 4) + unit // 4, unit % 4 * 4

    def add(step, unit, target, value):
        sums[target] = value if unit % 4 == 0 else sums[target] + value

    list_steps(HERE * 4 // UNITS, choose, far_ids, far_sources, far_charge, far_targets, squares, add)

    def far_store(i, carry):
        far_out[:, pl.ds(pl.multiple_of(i * 128, 128), 128)] = folded(sums, i)
        return carry

    lax.fori_loop(0, HERE // 2, far_store, 0)


def last_kernel(
    device_far, rows, device_skeleton, branch_skeleton, branch_transfer, transfer, basis, near, far, out
):
    top, leaf = lax.axis_index("top"), lax.axis_index("leaf")
    same = lax.broadcasted_iota(jnp.int32, (LEAF, LEAF), 0) == lax.broadcasted_iota(
        jnp.int32, (LEAF, LEAF), 1
    )

    def upright(coords):
        return [
            jnp.sum(jnp.where(same, coords[i : i + 1], 0.0), axis=1, keepdims=True) for i in range(3)
        ]

    def block(own, other):
        total = 0.0
        for i in range(3):
            differ = own[i] - other[i : i + 1]
            total = total + differ * differ
        scaled = KERNEL_SCALE * jnp.sqrt(total)
        return SIGNAL * (1.0 + scaled) * jnp.exp(-scaled)

    def exact(a, b, dims):
        return lax.dot_general(a, b, dims, precision=EXACT, preferred_element_type=F32)

    own = upright(device_skeleton[top * 16 + leaf])
    coupled = jnp.zeros((RHS, LEAF), F32)
    for k in range(4):
        partner = jnp.minimum(jnp.maximum(device_far[k, 0], 0), 127)
        coupled = coupled + exact(rows[partner][:, :LEAF], block(own, device_skeleton[partner]), NT)
    own = upright(branch_skeleton[top])
    field = jnp.zeros((RHS, LEAF), F32)
    for e in range(8):
        total = rows[16 * e]
        for d in range(1, 16):
            total = total + rows[16 * e + d]
        weight = jnp.where(jnp.abs(e - top) >= 2, 1.0, 0.0)
        field = field + exact(total[:, LEAF:] * weight, block(own, branch_skeleton[e]), NT)
    coupled = coupled + exact(field, branch_transfer[...], NN)
    lifted = jnp.concatenate(halves(coupled), axis=0)
    half = low_lanes(RHS)
    together = 4

    def step(index, carry):
        places, fields = [], []
        for part in range(together):
            place = pl.ds(pl.multiple_of((index * together + part) * 256, 256), 256)
            t_high, t_low = halves(transfer[:, place])
            up = dot(lifted, t_high) + dot(lifted, t_low)
            places.append(place)
            fields.append(far[:, place] + (up[:RHS] + up[RHS:]))
        products = []
        for place, value in zip(places, fields):
            pieces = []
            for i in range(4):
                tile = value[:, (i // 2) * 128 : (i // 2) * 128 + 128]
                tile = jnp.where(half, tile, 0.0) if i % 2 == 0 else jnp.where(half, 0.0, tile)
                pieces.extend(halves(tile))
            lines = jnp.concatenate(pieces, axis=0)
            b_high, b_low = halves(basis[:, place])
            products.append(
                dot(lines, jnp.concatenate([b_high, b_high], axis=0))
                + dot(lines, jnp.concatenate([b_low, b_low], axis=0))
            )
        for place, product in zip(places, products):
            each = [product[32 * i : 32 * i + 16] + product[32 * i + 16 : 32 * i + 32] for i in range(4)]
            result = jnp.concatenate(
                [
                    jnp.where(half, each[0][:, :128], each[1][:, :128]),
                    jnp.where(half, each[2][:, 128:], each[3][:, 128:]),
                ],
                axis=1,
            )
            out[:, place] = near[:, place] + result
        return carry

    lax.fori_loop(0, HERE // 4 // together, step, 0)


def shape(*dims, dtype=F32):
    return jax.ShapeDtypeStruct(dims, dtype)


def body(
    points,
    charges,
    near_list,
    far_list,
    leaf_basis,
    transfer,
    leaf_skeleton,
    device_far,
    branch_transfer,
    device_skeleton,
    branch_skeleton,
):
    here = charges.shape[1]

    def moved(array, axis, up):
        size = lax.axis_size(axis)
        pairs = [(i, i + 1) for i in range(size - 1)]
        return lax.ppermute(array, axis, pairs if up else [(j, i) for i, j in pairs])

    coef, device_row, near_ids, far_ids, work, send_down, send_up = pl.pallas_call(
        first_kernel,
        in_specs=[VMEM] * 8,
        out_specs=[VMEM] * 7,
        out_shape=[
            shape(RHS, here), shape(RHS, 128), shape(32, HERE, dtype=jnp.int32), shape(FAR, HERE, dtype=jnp.int32),
            shape(8, 512, dtype=jnp.int32), shape(ROWS, YCOLS * COL), shape(ROWS, YCOLS * COL),
        ],
        compiler_params=PARAMS,
        name="coefficients",
    )(points, charges, near_list, far_list, leaf_basis, transfer, leaf_skeleton, branch_transfer)
    every_row = lax.all_gather(device_row, ("top", "leaf"), axis=0)
    from_down = moved(send_up, "leaf", True)
    from_up = moved(send_down, "leaf", False)

    def scratch(leaves):
        return [
            pltpu.VMEM((leaves, 32, 128), BF16),
            pltpu.VMEM((leaves, 32, 128), BF16),
            pltpu.VMEM((HERE, LEAF, 32), BF16),
        ]

    common = [pltpu.VMEM((UNITS, LEAF, 4 * LEAF), F32), pltpu.VMEM((HERE, RHS, 128), F32)]

    def cost(us):
        return pl.CostEstimate(flops=us * 10**9, bytes_accessed=10**6, transcendentals=0)

    inner = pl.pallas_call(
        inner_kernel,
        in_specs=[SMEM] * 2 + [VMEM] * 2,
        out_specs=VMEM,
        out_shape=shape(RHS, 4 * COL),
        scratch_shapes=scratch(NEAR_NULL + 1) + common,
        compiler_params=PARAMS,
        cost_estimate=cost(13),
        name="inner",
    )(near_ids, work, points, charges)
    send_left, send_right = pl.pallas_call(
        side_kernel,
        in_specs=[VMEM] * 6,
        out_specs=[VMEM] * 2,
        out_shape=[shape(ROWS, XCOLS * COL), shape(ROWS, XCOLS * COL)],
        compiler_params=PARAMS,
        name="sides",
    )(points, charges, leaf_skeleton, coef, from_down, from_up)
    from_left = moved(send_right, "top", True)
    from_right = moved(send_left, "top", False)
    strip = pl.pallas_call(
        strip_kernel,
        in_specs=[SMEM] * 2 + [VMEM] * 4,
        out_specs=VMEM,
        out_shape=shape(RHS, 4 * COL),
        scratch_shapes=scratch(NEAR_NULL + 1) + common,
        compiler_params=PARAMS,
        cost_estimate=cost(13),
        name="strip",
    )(near_ids, work, points, charges, from_down, from_up)
    near, far = pl.pallas_call(
        rest_kernel,
        in_specs=[SMEM] * 3 + [VMEM] * 10,
        out_specs=[VMEM] * 2,
        out_shape=[shape(RHS, here), shape(RHS, here)],
        scratch_shapes=scratch(NEAR_NULL + 1) + scratch(FAR_ALL) + common,
        compiler_params=PARAMS,
        cost_estimate=cost(55),
        name="rest",
    )(
        near_ids, work, far_ids, points, charges, leaf_skeleton, coef, from_down, from_up, from_left, from_right,
        inner, strip,
    )
    return pl.pallas_call(
        last_kernel,
        in_specs=[SMEM] + [VMEM] * 8,
        out_specs=VMEM,
        out_shape=shape(RHS, here),
        compiler_params=PARAMS,
        name="fields",
    )(
        device_far,
        every_row,
        device_skeleton.reshape(3, -1, LEAF).transpose(1, 0, 2),
        branch_skeleton.reshape(3, -1, LEAF).transpose(1, 0, 2),
        branch_transfer,
        transfer,
        leaf_basis,
        near,
        far,
    )


def solution(mesh):
    split = P(None, ("top", "leaf"))
    return jax.shard_map(
        body, mesh=mesh, in_specs=(split,) * 9 + (P(), P()), out_specs=split, check_vma=False
    )
```

```python
import jax
import jax.numpy as jnp
from jax import lax
from jax.experimental import pallas as pl
from jax.experimental.pallas import tpu as pltpu
from jax.sharding import PartitionSpec as P

LEAF = 64
RANK = 64
RHS = 16
BX = 4
BY = 4
BZ = 8
COLS = BX * BY
COL = BZ * LEAF
HERE = COLS * BZ
NEAR = 27
FAR = 16
NX = BX + 2
FX = BX + 4
NEAR_NULL = NX * NX * BZ
FAR_ALL = FX * FX * BZ
YFAR, YNEAR = 2 * BX, BX
XFAR, XNEAR = 2 * FX, NX
YCOLS = YFAR + YNEAR
XCOLS = XFAR + XNEAR
YLANES = (YCOLS + (YCOLS + 3) // 4) * COL
XLANES = (XCOLS + (XCOLS + 3) // 4) * COL
UNITS = 32
BLOCK = 1024
INNER = ((1, 1), (1, 2), (2, 1), (2, 2))
STRIP = ((1, 0), (1, 3), (2, 0), (2, 3))
RIM = tuple((x, y) for x in (0, 3) for y in range(4))

EXACT = lax.Precision.HIGHEST
KERNEL_SCALE = 3.4641016151377544
LOG2E = 1.4426950408889634
SIGNAL = 0.0625
NUGGET = 0.25
BF16 = jnp.bfloat16
F32 = jnp.float32
NT = (((1,), (1,)), ((), ()))
NN = (((1,), (0,)), ((), ()))
VMEM = pl.BlockSpec(memory_space=pltpu.VMEM)
SMEM = pl.BlockSpec(memory_space=pltpu.SMEM)


def room(mib):
    return pltpu.CompilerParams(vmem_limit_bytes=mib * 2**20)


def dot(a, b, dims=NN):
    return lax.dot_general(a, b, dims, preferred_element_type=F32)


def halves(value):
    high = value.astype(BF16)
    return high, (value - high.astype(F32)).astype(BF16)


def low_lanes(rows):
    return lax.broadcasted_iota(jnp.int32, (rows, 128), 1) < LEAF


def column(index):
    return pl.ds(pl.multiple_of(index * COL, COL), COL)


def coords_at(array, columns, index, odd):
    row = pl.ds(pl.multiple_of(index // 2 % 2 * 8, 8), 8)
    return array[row, column(columns + index // 4)][3 * odd : 3 * odd + 3]


def set_coords(array, columns, index, value):
    row = index // 2 % 2 * 8 + index % 2 * 3
    array[row : row + 3, column(columns + index // 4)] = value


def window_ids(ids, width, span, top, leaf, null):
    wx = ((ids >> 11) - top) * BX + ((ids >> 5) & 3) + width
    wy = (((ids >> 7) & 15) - leaf) * BY + ((ids >> 3) & 3) + width
    place = (wx * span + wy) * BZ + (ids & 7)
    place = jnp.minimum(jnp.maximum(place, 0), span * span * BZ - 1)
    return jnp.where(ids >= 0, place, null)


def work_lists(used, work):
    lane = lax.broadcasted_iota(jnp.int32, (1, HERE), 1)
    inner_x = (((lane >> 5) + 1) & 2) != 0
    inner_y = ((((lane >> 3) & 3) + 1) & 2) != 0
    member = jnp.where(inner_x, jnp.where(inner_y, 0, 1), 2)
    parts = (used + 3) >> 2
    first = lax.broadcasted_iota(jnp.int32, (HERE, HERE), 0)
    second = lax.broadcasted_iota(jnp.int32, (HERE, HERE), 1)
    place = lax.broadcasted_iota(jnp.int32, (HERE, 512), 1)
    for phase in range(3):
        kept = jnp.where(member == phase, parts, 0)
        end = jnp.sum(jnp.where(second <= first, kept, 0), axis=1, keepdims=True)
        count = jnp.sum(jnp.where(second == first, kept, 0), axis=1, keepdims=True)
        passed = end <= place
        leaf = jnp.sum(jnp.where(passed, 1, 0), axis=0, keepdims=True)
        start = jnp.sum(jnp.where(passed, count, 0), axis=0, keepdims=True)
        code = leaf * 8 + (place[:1] - start)
        work[phase : phase + 1] = jnp.where(leaf < HERE, code, 7)
        work[4 + phase : 5 + phase] = jnp.zeros((1, 512), jnp.int32) + jnp.sum(kept, axis=1, keepdims=True)


def first_kernel(
    points, charges, near_list, far_list, basis, transfer, skeleton, branch_transfer,
    coef, device_row, near_ids, far_ids, work, send_down, send_up, total,
):
    lane = lax.broadcasted_iota(jnp.int32, (2 * RHS, 4 * LEAF), 1) // LEAF
    half = low_lanes(RHS)
    together = BLOCK // 256
    index = pl.program_id(0)

    places, products = [], []
    for part in range(together):
        place = pl.ds(pl.multiple_of(index * BLOCK + part * 256, 256), 256)
        here = slice(part * 256, part * 256 + 256)
        places.append((place, here))
        q_high, q_low = halves(charges[:, place])
        q = jnp.concatenate([q_high, q_low], axis=0)
        zero = jnp.zeros_like(q)
        rows = jnp.concatenate([jnp.where(lane == i, q, zero) for i in range(4)], axis=0)
        b_high, b_low = halves(basis[:, here])
        products.append(
            dot(rows, jnp.concatenate([b_high, b_high], axis=0), NT)
            + dot(rows, jnp.concatenate([b_low, b_low], axis=0), NT)
        )
    sums = []
    for (place, here), product in zip(places, products):
        each = [product[32 * i : 32 * i + 16] + product[32 * i + 16 : 32 * i + 32] for i in range(4)]
        value = jnp.concatenate(
            [jnp.where(half, each[0], each[1]), jnp.where(half, each[2], each[3])], axis=1
        )
        coef[:, place] = value
        c = jnp.concatenate(halves(value), axis=0)
        t_high, t_low = halves(transfer[:, here])
        sums.append(dot(c, t_high, NT) + dot(c, t_low, NT))

    @pl.when(index == 0)
    def start():
        total[...] = jnp.zeros((2 * RHS, LEAF), F32)

    total[...] = total[...] + sum(sums[1:], sums[0])

    @pl.when(index == HERE * LEAF // BLOCK - 1)
    def finish():
        top, leaf = lax.axis_index("top"), lax.axis_index("leaf")
        listed = near_list[...]
        near_ids[0:NEAR] = window_ids(listed, 1, NX, top, leaf, NEAR_NULL)
        near_ids[NEAR:32] = jnp.full((5, HERE), NEAR_NULL, jnp.int32)
        work_lists(jnp.sum((listed >= 0).astype(jnp.int32), axis=0, keepdims=True), work)
        far_ids[...] = window_ids(far_list[...], 2, FX, top, leaf, 0)

        own = total[0:RHS] + total[RHS : 2 * RHS]
        raised = lax.dot_general(own, branch_transfer[...], NT, precision=EXACT, preferred_element_type=F32)
        device_row[...] = jnp.concatenate([own, raised], axis=1)

        def fill(target, near_y, far_y):
            for x in range(BX):
                for y in range(2):
                    at = column(x * BY + far_y + y)
                    target[:, column(x * 2 + y)] = coef[:, at]
                    set_coords(target, YCOLS, x * 2 + y, skeleton[:, at])
                at = column(x * BY + near_y)
                target[:, column(YFAR + x)] = charges[:, at]
                set_coords(target, YCOLS, YFAR + x, points[:, at])

        blank = jnp.zeros((RHS, YLANES - YCOLS * COL), F32)
        send_down[:, YCOLS * COL : YLANES] = blank
        send_up[:, YCOLS * COL : YLANES] = blank
        fill(send_down, 0, 0)
        fill(send_up, BY - 1, BY - 2)


def side_kernel(points, charges, skeleton, coef, from_down, from_up, send_left, send_right):
    def fill(target, near_x, far_x):
        def put(index, values, coords):
            target[:, column(index)] = values
            set_coords(target, XCOLS, index, coords)

        def side(index, array, at):
            put(index, array[:, column(at)], coords_at(array, YCOLS, at, at % 2))

        for x in range(2):
            at_x = far_x + x
            for y in range(2):
                side(x * FX + y, from_down, at_x * 2 + y)
                side(x * FX + y + BY + 2, from_up, at_x * 2 + y)
            for y in range(BY):
                at = column(at_x * BY + y)
                put(x * FX + 2 + y, coef[:, at], skeleton[:, at])
        side(XFAR, from_down, YFAR + near_x)
        side(XFAR + BY + 1, from_up, YFAR + near_x)
        for y in range(BY):
            at = column(near_x * BY + y)
            put(XFAR + 1 + y, charges[:, at], points[:, at])

    blank = jnp.zeros((RHS, XLANES - XCOLS * COL), F32)
    send_left[:, XCOLS * COL : XLANES] = blank
    send_right[:, XCOLS * COL : XLANES] = blank
    fill(send_left, 0, 0)
    fill(send_right, BX - 1, BX - 2)


def pieces_of(coords, centre):
    place = (coords - centre) * KERNEL_SCALE
    high = place.astype(BF16).astype(F32)
    rest = place - high
    mid = rest.astype(BF16).astype(F32)
    norm = jnp.sum(place * place, axis=0, keepdims=True)
    norm_high = norm.astype(BF16).astype(F32)
    norm_rest = norm - norm_high
    norm_mid = norm_rest.astype(BF16).astype(F32)
    return high, mid, rest - mid, norm_high, norm_mid, norm_rest - norm_mid


def build_column(coords, values, centre, col, sources, charge):
    high, mid, low, norm_high, norm_mid, norm_low = pieces_of(coords, centre)
    one = jnp.ones_like(norm_high)
    empty = jnp.zeros((8, 128), BF16)
    rows = jnp.concatenate([high, high, norm_high, norm_mid, high, mid, norm_low, one, mid, low, one, one], axis=0)
    half = low_lanes(24)
    half_values = low_lanes(RHS)
    scaled = values * SIGNAL
    for pair in range(BZ // 2):
        lanes = slice(pair * 128, pair * 128 + 128)
        tile, tile_values = rows[:, lanes], scaled[:, lanes]
        turned, turned_values = pltpu.roll(tile, LEAF, 1), pltpu.roll(tile_values, LEAF, 1)
        at = col * BZ + 2 * pair
        sources[at] = jnp.concatenate([jnp.where(half, tile, turned).astype(BF16), empty], axis=0)
        sources[at + 1] = jnp.concatenate([jnp.where(half, turned, tile).astype(BF16), empty], axis=0)
        charge[at] = jnp.concatenate(halves(jnp.where(half_values, tile_values, turned_values)), axis=0)
        charge[at + 1] = jnp.concatenate(halves(jnp.where(half_values, turned_values, tile_values)), axis=0)


def build_targets(coords, centre, targets, leaf):
    high, mid, low, norm_high, norm_mid, norm_low = pieces_of(coords, centre)
    one = jnp.ones_like(norm_high)
    rows = jnp.concatenate(
        [
            -2.0 * high, -2.0 * mid, one, one, -2.0 * low, -2.0 * high, one, norm_high,
            -2.0 * mid, -2.0 * high, norm_mid, norm_low, jnp.zeros((8, COL), F32),
        ],
        axis=0,
    )
    for pair in range(BZ // 2):
        tile = rows[:, pair * 128 : pair * 128 + 128].T.astype(BF16)
        targets[leaf + 2 * pair] = tile[:LEAF]
        targets[leaf + 2 * pair + 1] = tile[LEAF:]


def centre_of():
    top, leaf = lax.axis_index("top"), lax.axis_index("leaf")
    row = lax.broadcasted_iota(jnp.int32, (3, COL), 0)
    return jnp.where(row == 0, top.astype(F32) + 0.5, jnp.where(row == 1, leaf.astype(F32) + 0.5, 1.0))


def region(array, columns, first, count, to, centre, sources, charge):
    def step(half, carry):
        for odd in range(2):
            i = 2 * half + odd
            coords = coords_at(array, columns, first + i, odd)
            build_column(coords, array[:, column(first + i)], centre, to(i), sources, charge)
        return carry

    lax.fori_loop(0, count // 2, step, 0)


def own_columns(coords, values, to, centre, sources, charge):
    def step(half, carry):
        for i in (2 * half, 2 * half + 1):
            at = column(i)
            build_column(coords[:, at], values[:, at], centre, to(i), sources, charge)
        return carry

    lax.fori_loop(0, COLS // 2, step, 0)


def gathered(array, ids, slot, target):
    half = low_lanes(32)
    four = [array[ids[slot + k, target]] for k in range(4)]
    return jnp.concatenate([jnp.where(half, four[0], four[1]), jnp.where(half, four[2], four[3])], axis=1)


def entries_of(square):
    square = jnp.maximum(square, 1e-20)
    scaled = square * lax.rsqrt(square)
    decay = jnp.exp2(scaled * -LOG2E)
    return jnp.concatenate(halves(decay + scaled * decay), axis=0)


def list_steps(steps, choose, ids, sources, charge, targets, squares, add):
    def distances(step, unit):
        target, slot = choose(step, unit)
        squares[unit] = dot(targets[target], gathered(sources, ids, slot, target))

    for unit in range(UNITS):
        distances(0, unit)

    def run(step, carry):
        waiting = None
        for unit in range(UNITS + 1):
            if unit < UNITS:
                entries = entries_of(squares[unit])
                distances(jnp.minimum(step + 1, steps - 1), unit)
            if waiting is not None:
                target, slot = choose(step, unit - 1)
                product = dot(gathered(charge, ids, slot, target), waiting, NT)
                add(step, unit - 1, target, product[:RHS] + product[RHS:])
            waiting = entries
        return carry

    lax.fori_loop(0, steps, run, 0)


def near_pass(phase, cells, near_ids, work, points, centre, sources, charge, targets, squares, sums):
    for x, y in cells:
        col = x * BY + y
        build_targets(points[:, col * COL : col * COL + COL], centre, targets, col * BZ)

        def zero(i, carry, first=col * BZ):
            sums[first + i] = jnp.zeros((RHS, 128), F32)
            return carry

        lax.fori_loop(0, BZ, zero, 0)
    sources[NEAR_NULL] = jnp.zeros((32, 128), BF16)
    charge[NEAR_NULL] = jnp.zeros((32, 128), BF16)

    def choose(step, unit):
        code = work[phase, step * UNITS + unit]
        return code >> 3, (code & 7) * 4

    def add(step, unit, target, value):
        sums[target] = sums[target] + value

    steps = jnp.maximum((work[4 + phase, 0] + UNITS - 1) // UNITS, 1)
    list_steps(steps, choose, near_ids, sources, charge, targets, squares, add)


def folded(sums, pair):
    first, second = sums[2 * pair], sums[2 * pair + 1]
    first = first + pltpu.roll(first, LEAF, 1)
    second = second + pltpu.roll(second, LEAF, 1)
    return jnp.where(low_lanes(RHS), first, second)


def near_store(cells, out, places, sums, charges):
    for (x, y), to in zip(cells, places):
        for pair in range(BZ // 2):
            at = (x * BY + y) * COL + pair * 128
            value = folded(sums, (x * BY + y) * (BZ // 2) + pair)
            out[:, to * COL + pair * 128 : to * COL + pair * 128 + 128] = value + NUGGET * charges[:, at : at + 128]


def near_own(points, charges, centre, sources, charge):
    own_columns(points, charges, lambda i: (i // BY + 1) * NX + i % BY + 1, centre, sources, charge)


def near_sides(from_down, from_up, centre, sources, charge):
    region(from_down, YCOLS, YFAR, YNEAR, lambda i: (i + 1) * NX, centre, sources, charge)
    region(from_up, YCOLS, YFAR, YNEAR, lambda i: (i + 1) * NX + NX - 1, centre, sources, charge)


def inner_kernel(near_ids, work, points, charges, out, sources, charge, targets, squares, sums):
    centre = centre_of()
    near_own(points, charges, centre, sources, charge)
    near_pass(0, INNER, near_ids, work, points, centre, sources, charge, targets, squares, sums)
    near_store(INNER, out, range(4), sums, charges)


def strip_kernel(
    near_ids, work, points, charges, from_down, from_up, out, sources, charge, targets, squares, sums
):
    centre = centre_of()
    near_own(points, charges, centre, sources, charge)
    near_sides(from_down, from_up, centre, sources, charge)
    near_pass(1, STRIP, near_ids, work, points, centre, sources, charge, targets, squares, sums)
    near_store(STRIP, out, range(4), sums, charges)


def rest_kernel(
    near_ids, work, far_ids, points, charges, skeleton, coef, from_down, from_up, from_left, from_right,
    inner, strip, near_out, far_out,
    sources, charge, targets, far_sources, far_charge, far_targets, squares, sums,
):
    centre = centre_of()
    near_own(points, charges, centre, sources, charge)
    near_sides(from_down, from_up, centre, sources, charge)
    region(from_left, XCOLS, XFAR, XNEAR, lambda i: i, centre, sources, charge)
    region(from_right, XCOLS, XFAR, XNEAR, lambda i: (NX - 1) * NX + i, centre, sources, charge)
    near_pass(2, RIM, near_ids, work, points, centre, sources, charge, targets, squares, sums)
    near_store(RIM, near_out, [x * BY + y for x, y in RIM], sums, charges)
    for cells, done in ((INNER, inner), (STRIP, strip)):
        for i, (x, y) in enumerate(cells):
            near_out[:, column(x * BY + y)] = done[:, i * COL : i * COL + COL]

    own_columns(
        skeleton, coef, lambda i: (i // BY + 2) * FX + i % BY + 2, centre, far_sources, far_charge
    )

    def target_step(i, carry):
        build_targets(skeleton[:, column(i)], centre, far_targets, i * BZ)
        return carry

    lax.fori_loop(0, COLS, target_step, 0)
    region(from_down, YCOLS, 0, YFAR, lambda i: (i // 2 + 2) * FX + i % 2, centre, far_sources, far_charge)
    region(from_up, YCOLS, 0, YFAR, lambda i: (i // 2 + 2) * FX + i % 2 + BY + 2, centre, far_sources, far_charge)
    region(from_left, XCOLS, 0, XFAR, lambda i: i, centre, far_sources, far_charge)
    region(from_right, XCOLS, 0, XFAR, lambda i: (BX + 2) * FX + i, centre, far_sources, far_charge)

    def choose(step, unit):
        return step * (UNITS // 4) + unit // 4, unit % 4 * 4

    def add(step, unit, target, value):
        sums[target] = value if unit % 4 == 0 else sums[target] + value

    list_steps(HERE * 4 // UNITS, choose, far_ids, far_sources, far_charge, far_targets, squares, add)

    def far_store(i, carry):
        far_out[:, pl.ds(pl.multiple_of(i * 128, 128), 128)] = folded(sums, i)
        return carry

    lax.fori_loop(0, HERE // 2, far_store, 0)


def last_kernel(
    device_far, rows, device_skeleton, branch_skeleton, branch_transfer, transfer, basis, near, far, out, coupling
):
    @pl.when(pl.program_id(0) == 0)
    def start():
        top, leaf = lax.axis_index("top"), lax.axis_index("leaf")
        same = lax.broadcasted_iota(jnp.int32, (LEAF, LEAF), 0) == lax.broadcasted_iota(
            jnp.int32, (LEAF, LEAF), 1
        )

        def upright(coords):
            return [
                jnp.sum(jnp.where(same, coords[i : i + 1], 0.0), axis=1, keepdims=True) for i in range(3)
            ]

        def kernel_block(own, other):
            total = 0.0
            for i in range(3):
                differ = own[i] - other[i : i + 1]
                total = total + differ * differ
            scaled = KERNEL_SCALE * jnp.sqrt(total)
            return SIGNAL * (1.0 + scaled) * jnp.exp(-scaled)

        def exact(a, b, dims):
            return lax.dot_general(a, b, dims, precision=EXACT, preferred_element_type=F32)

        def cluster(skeletons, index):
            tile = skeletons[:, pl.ds(pl.multiple_of(index // 2 * 128, 128), 128)]
            return jnp.where(index % 2 == 0, tile, pltpu.roll(tile, LEAF, 1))[:, :LEAF]

        own = upright(cluster(device_skeleton, top * 16 + leaf))
        coupled = jnp.zeros((RHS, LEAF), F32)
        for k in range(4):
            partner = jnp.minimum(jnp.maximum(device_far[k, 0], 0), 127)
            coupled = coupled + exact(rows[partner][:, :LEAF], kernel_block(own, cluster(device_skeleton, partner)), NT)
        own = upright(cluster(branch_skeleton, top))
        field = jnp.zeros((RHS, LEAF), F32)
        for e in range(8):
            total = rows[16 * e]
            for d in range(1, 16):
                total = total + rows[16 * e + d]
            weight = jnp.where(jnp.abs(e - top) >= 2, 1.0, 0.0)
            field = field + exact(total[:, LEAF:] * weight, kernel_block(own, cluster(branch_skeleton, e)), NT)
        coupled = coupled + exact(field, branch_transfer[...], NN)
        coupling[...] = coupled

    lifted = jnp.concatenate(halves(coupling[...]), axis=0)
    half = low_lanes(RHS)
    together = BLOCK // 256

    places, fields = [], []
    for part in range(together):
        place = slice(part * 256, part * 256 + 256)
        t_high, t_low = halves(transfer[:, place])
        up = dot(lifted, t_high) + dot(lifted, t_low)
        places.append(place)
        fields.append(far[:, place] + (up[:RHS] + up[RHS:]))
    products = []
    for place, value in zip(places, fields):
        pieces = []
        for i in range(4):
            tile = value[:, (i // 2) * 128 : (i // 2) * 128 + 128]
            tile = jnp.where(half, tile, 0.0) if i % 2 == 0 else jnp.where(half, 0.0, tile)
            pieces.extend(halves(tile))
        lines = jnp.concatenate(pieces, axis=0)
        b_high, b_low = halves(basis[:, place])
        products.append(
            dot(lines, jnp.concatenate([b_high, b_high], axis=0))
            + dot(lines, jnp.concatenate([b_low, b_low], axis=0))
        )
    for place, product in zip(places, products):
        each = [product[32 * i : 32 * i + 16] + product[32 * i + 16 : 32 * i + 32] for i in range(4)]
        result = jnp.concatenate(
            [
                jnp.where(half, each[0][:, :128], each[1][:, :128]),
                jnp.where(half, each[2][:, 128:], each[3][:, 128:]),
            ],
            axis=1,
        )
        out[:, place] = near[:, place] + result


def block(rows):
    return pl.BlockSpec((rows, BLOCK), lambda i: (0, i))


def shape(*dims, dtype=F32):
    return jax.ShapeDtypeStruct(dims, dtype)


def body(
    points,
    charges,
    near_list,
    far_list,
    leaf_basis,
    transfer,
    leaf_skeleton,
    device_far,
    branch_transfer,
    device_skeleton,
    branch_skeleton,
):
    here = charges.shape[1]

    def moved(array, axis, up):
        size = lax.axis_size(axis)
        pairs = [(i, i + 1) for i in range(size - 1)]
        return lax.ppermute(array, axis, pairs if up else [(j, i) for i, j in pairs])

    coef, device_row, near_ids, far_ids, work, send_down, send_up = pl.pallas_call(
        first_kernel,
        grid=(here // BLOCK,),
        in_specs=[VMEM] * 4 + [block(RANK)] * 2 + [VMEM] * 2,
        out_specs=[VMEM] * 7,
        scratch_shapes=[pltpu.VMEM((2 * RHS, LEAF), F32)],
        out_shape=[
            shape(RHS, here), shape(RHS, 128), shape(32, HERE, dtype=jnp.int32), shape(FAR, HERE, dtype=jnp.int32),
            shape(8, 512, dtype=jnp.int32), shape(RHS, YLANES), shape(RHS, YLANES),
        ],
        compiler_params=room(60),
        name="coefficients",
    )(points, charges, near_list, far_list, leaf_basis, transfer, leaf_skeleton, branch_transfer)
    every_row = lax.all_gather(device_row, ("top", "leaf"), axis=0)
    from_down = moved(send_up, "leaf", True)
    from_up = moved(send_down, "leaf", False)

    def scratch(leaves):
        return [
            pltpu.VMEM((leaves, 32, 128), BF16),
            pltpu.VMEM((leaves, 32, 128), BF16),
            pltpu.VMEM((HERE, LEAF, 32), BF16),
        ]

    common = [pltpu.VMEM((UNITS, LEAF, 4 * LEAF), F32), pltpu.VMEM((HERE, RHS, 128), F32)]

    def cost(us):
        return pl.CostEstimate(flops=us * 10**9, bytes_accessed=10**6, transcendentals=0)

    inner = pl.pallas_call(
        inner_kernel,
        in_specs=[SMEM] * 2 + [VMEM] * 2,
        out_specs=VMEM,
        out_shape=shape(RHS, 4 * COL),
        scratch_shapes=scratch(NEAR_NULL + 1) + common,
        compiler_params=room(16),
        cost_estimate=cost(13),
        name="inner",
    )(near_ids, work, points, charges)
    send_left, send_right = pl.pallas_call(
        side_kernel,
        in_specs=[VMEM] * 6,
        out_specs=[VMEM] * 2,
        out_shape=[shape(RHS, XLANES), shape(RHS, XLANES)],
        compiler_params=room(12),
        name="sides",
    )(points, charges, leaf_skeleton, coef, from_down, from_up)
    from_left = moved(send_right, "top", True)
    from_right = moved(send_left, "top", False)
    strip = pl.pallas_call(
        strip_kernel,
        in_specs=[SMEM] * 2 + [VMEM] * 4,
        out_specs=VMEM,
        out_shape=shape(RHS, 4 * COL),
        scratch_shapes=scratch(NEAR_NULL + 1) + common,
        compiler_params=room(16),
        cost_estimate=cost(13),
        name="strip",
    )(near_ids, work, points, charges, from_down, from_up)
    near, far = pl.pallas_call(
        rest_kernel,
        in_specs=[SMEM] * 3 + [VMEM] * 10,
        out_specs=[VMEM] * 2,
        out_shape=[shape(RHS, here), shape(RHS, here)],
        scratch_shapes=scratch(NEAR_NULL + 1) + scratch(FAR_ALL) + common,
        compiler_params=room(30),
        cost_estimate=cost(55),
        name="rest",
    )(
        near_ids, work, far_ids, points, charges, leaf_skeleton, coef, from_down, from_up, from_left, from_right,
        inner, strip,
    )
    return pl.pallas_call(
        last_kernel,
        grid=(here // BLOCK,),
        in_specs=[SMEM] + [VMEM] * 4 + [block(RANK)] * 2 + [block(RHS)] * 2,
        out_specs=block(RHS),
        scratch_shapes=[pltpu.VMEM((RHS, LEAF), F32)],
        out_shape=shape(RHS, here),
        compiler_params=room(60),
        name="fields",
    )(
        device_far,
        every_row,
        device_skeleton,
        branch_skeleton,
        branch_transfer,
        transfer,
        leaf_basis,
        near,
        far,
    )


def solution(mesh):
    split = P(None, ("top", "leaf"))
    return jax.shard_map(
        body, mesh=mesh, in_specs=(split,) * 9 + (P(), P()), out_specs=split, check_vma=False
    )
```

```python
import jax
import jax.numpy as jnp
from jax import lax
from jax.experimental import pallas as pl
from jax.experimental.pallas import tpu as pltpu
from jax.sharding import PartitionSpec as P

LEAF = 64
RANK = 64
RHS = 16
BX = 4
BY = 4
BZ = 8
COLS = BX * BY
COL = BZ * LEAF
HERE = COLS * BZ
NEAR = 27
FAR = 16
NX = BX + 2
FX = BX + 4
NEAR_NULL = NX * NX * BZ
FAR_ALL = FX * FX * BZ
YFAR, YNEAR = 2 * BX, BX
XFAR, XNEAR = 2 * FX, NX
YCOLS = YFAR + YNEAR
XCOLS = XFAR + XNEAR
YLANES = (YCOLS + (YCOLS + 3) // 4) * COL
XLANES = (XCOLS + (XCOLS + 3) // 4) * COL
UNITS = 32
BLOCK = 2048
INNER = ((1, 1), (1, 2), (2, 1), (2, 2))
STRIP = ((1, 0), (1, 3), (2, 0), (2, 3))
RIM = tuple((x, y) for x in (0, 3) for y in range(4))

EXACT = lax.Precision.HIGHEST
KERNEL_SCALE = 3.4641016151377544
LOG2E = 1.4426950408889634
SIGNAL = 0.0625
NUGGET = 0.25
BF16 = jnp.bfloat16
F32 = jnp.float32
NT = (((1,), (1,)), ((), ()))
NN = (((1,), (0,)), ((), ()))
VMEM = pl.BlockSpec(memory_space=pltpu.VMEM)
SMEM = pl.BlockSpec(memory_space=pltpu.SMEM)


def room(mib):
    return pltpu.CompilerParams(vmem_limit_bytes=mib * 2**20)


def dot(a, b, dims=NN):
    return lax.dot_general(a, b, dims, preferred_element_type=F32)


def halves(value):
    high = value.astype(BF16)
    return high, (value - high.astype(F32)).astype(BF16)


def low_lanes(rows):
    return lax.broadcasted_iota(jnp.int32, (rows, 128), 1) < LEAF


def column(index):
    return pl.ds(pl.multiple_of(index * COL, COL), COL)


def coords_at(array, columns, index, odd):
    row = pl.ds(pl.multiple_of(index // 2 % 2 * 8, 8), 8)
    return array[row, column(columns + index // 4)][3 * odd : 3 * odd + 3]


def set_coords(array, columns, index, value):
    row = index // 2 % 2 * 8 + index % 2 * 3
    array[row : row + 3, column(columns + index // 4)] = value


def window_ids(ids, width, span, top, leaf, null):
    wx = ((ids >> 11) - top) * BX + ((ids >> 5) & 3) + width
    wy = (((ids >> 7) & 15) - leaf) * BY + ((ids >> 3) & 3) + width
    place = (wx * span + wy) * BZ + (ids & 7)
    place = jnp.minimum(jnp.maximum(place, 0), span * span * BZ - 1)
    return jnp.where(ids >= 0, place, null)


def work_lists(used, work):
    lane = lax.broadcasted_iota(jnp.int32, (1, HERE), 1)
    inner_x = (((lane >> 5) + 1) & 2) != 0
    inner_y = ((((lane >> 3) & 3) + 1) & 2) != 0
    member = jnp.where(inner_x, jnp.where(inner_y, 0, 1), 2)
    parts = (used + 3) >> 2
    first = lax.broadcasted_iota(jnp.int32, (HERE, HERE), 0)
    second = lax.broadcasted_iota(jnp.int32, (HERE, HERE), 1)
    place = lax.broadcasted_iota(jnp.int32, (HERE, 512), 1)
    for phase in range(3):
        kept = jnp.where(member == phase, parts, 0)
        end = jnp.sum(jnp.where(second <= first, kept, 0), axis=1, keepdims=True)
        count = jnp.sum(jnp.where(second == first, kept, 0), axis=1, keepdims=True)
        passed = end <= place
        leaf = jnp.sum(jnp.where(passed, 1, 0), axis=0, keepdims=True)
        start = jnp.sum(jnp.where(passed, count, 0), axis=0, keepdims=True)
        code = leaf * 8 + (place[:1] - start)
        work[phase : phase + 1] = jnp.where(leaf < HERE, code, 7)
        work[4 + phase : 5 + phase] = jnp.zeros((1, 512), jnp.int32) + jnp.sum(kept, axis=1, keepdims=True)


def first_kernel(
    points, charges, near_list, far_list, basis, transfer, skeleton, branch_transfer,
    coef, device_row, near_ids, far_ids, work, send_down, send_up, total,
):
    lane = lax.broadcasted_iota(jnp.int32, (2 * RHS, 4 * LEAF), 1) // LEAF
    half = low_lanes(RHS)
    together = BLOCK // 256
    index = pl.program_id(0)

    places, products = [], []
    for part in range(together):
        place = pl.ds(pl.multiple_of(index * BLOCK + part * 256, 256), 256)
        here = slice(part * 256, part * 256 + 256)
        places.append((place, here))
        q_high, q_low = halves(charges[:, place])
        q = jnp.concatenate([q_high, q_low], axis=0)
        zero = jnp.zeros_like(q)
        rows = jnp.concatenate([jnp.where(lane == i, q, zero) for i in range(4)], axis=0)
        b_high, b_low = halves(basis[:, here])
        products.append(
            dot(rows, jnp.concatenate([b_high, b_high], axis=0), NT)
            + dot(rows, jnp.concatenate([b_low, b_low], axis=0), NT)
        )
    sums = []
    for (place, here), product in zip(places, products):
        each = [product[32 * i : 32 * i + 16] + product[32 * i + 16 : 32 * i + 32] for i in range(4)]
        value = jnp.concatenate(
            [jnp.where(half, each[0], each[1]), jnp.where(half, each[2], each[3])], axis=1
        )
        coef[:, place] = value
        c = jnp.concatenate(halves(value), axis=0)
        t_high, t_low = halves(transfer[:, here])
        sums.append(dot(c, t_high, NT) + dot(c, t_low, NT))

    @pl.when(index == 0)
    def start():
        total[...] = jnp.zeros((2 * RHS, LEAF), F32)

    total[...] = total[...] + sum(sums[1:], sums[0])

    @pl.when(index == HERE * LEAF // BLOCK - 1)
    def finish():
        top, leaf = lax.axis_index("top"), lax.axis_index("leaf")
        listed = near_list[...]
        near_ids[0:NEAR] = window_ids(listed, 1, NX, top, leaf, NEAR_NULL)
        near_ids[NEAR:32] = jnp.full((5, HERE), NEAR_NULL, jnp.int32)
        work_lists(jnp.sum((listed >= 0).astype(jnp.int32), axis=0, keepdims=True), work)
        far_ids[...] = window_ids(far_list[...], 2, FX, top, leaf, 0)

        own = total[0:RHS] + total[RHS : 2 * RHS]
        raised = lax.dot_general(own, branch_transfer[...], NT, precision=EXACT, preferred_element_type=F32)
        device_row[...] = jnp.concatenate([own, raised], axis=1)

        def fill(target, near_y, far_y):
            for x in range(BX):
                for y in range(2):
                    at = column(x * BY + far_y + y)
                    target[:, column(x * 2 + y)] = coef[:, at]
                    set_coords(target, YCOLS, x * 2 + y, skeleton[:, at])
                at = column(x * BY + near_y)
                target[:, column(YFAR + x)] = charges[:, at]
                set_coords(target, YCOLS, YFAR + x, points[:, at])

        blank = jnp.zeros((RHS, YLANES - YCOLS * COL), F32)
        send_down[:, YCOLS * COL : YLANES] = blank
        send_up[:, YCOLS * COL : YLANES] = blank
        fill(send_down, 0, 0)
        fill(send_up, BY - 1, BY - 2)


def side_kernel(points, charges, skeleton, coef, from_down, from_up, send_left, send_right):
    def fill(target, near_x, far_x):
        def put(index, values, coords):
            target[:, column(index)] = values
            set_coords(target, XCOLS, index, coords)

        def side(index, array, at):
            put(index, array[:, column(at)], coords_at(array, YCOLS, at, at % 2))

        for x in range(2):
            at_x = far_x + x
            for y in range(2):
                side(x * FX + y, from_down, at_x * 2 + y)
                side(x * FX + y + BY + 2, from_up, at_x * 2 + y)
            for y in range(BY):
                at = column(at_x * BY + y)
                put(x * FX + 2 + y, coef[:, at], skeleton[:, at])
        side(XFAR, from_down, YFAR + near_x)
        side(XFAR + BY + 1, from_up, YFAR + near_x)
        for y in range(BY):
            at = column(near_x * BY + y)
            put(XFAR + 1 + y, charges[:, at], points[:, at])

    blank = jnp.zeros((RHS, XLANES - XCOLS * COL), F32)
    send_left[:, XCOLS * COL : XLANES] = blank
    send_right[:, XCOLS * COL : XLANES] = blank
    fill(send_left, 0, 0)
    fill(send_right, BX - 1, BX - 2)


def pieces_of(coords, centre):
    place = (coords - centre) * KERNEL_SCALE
    high = place.astype(BF16).astype(F32)
    rest = place - high
    mid = rest.astype(BF16).astype(F32)
    norm = jnp.sum(place * place, axis=0, keepdims=True)
    norm_high = norm.astype(BF16).astype(F32)
    norm_rest = norm - norm_high
    norm_mid = norm_rest.astype(BF16).astype(F32)
    return high, mid, rest - mid, norm_high, norm_mid, norm_rest - norm_mid


def build_column(coords, values, centre, col, sources, charge):
    high, mid, low, norm_high, norm_mid, norm_low = pieces_of(coords, centre)
    one = jnp.ones_like(norm_high)
    empty = jnp.zeros((8, 128), BF16)
    rows = jnp.concatenate([high, high, norm_high, norm_mid, high, mid, norm_low, one, mid, low, one, one], axis=0)
    half = low_lanes(24)
    half_values = low_lanes(RHS)
    scaled = values * SIGNAL
    for pair in range(BZ // 2):
        lanes = slice(pair * 128, pair * 128 + 128)
        tile, tile_values = rows[:, lanes], scaled[:, lanes]
        turned, turned_values = pltpu.roll(tile, LEAF, 1), pltpu.roll(tile_values, LEAF, 1)
        at = col * BZ + 2 * pair
        sources[at] = jnp.concatenate([jnp.where(half, tile, turned).astype(BF16), empty], axis=0)
        sources[at + 1] = jnp.concatenate([jnp.where(half, turned, tile).astype(BF16), empty], axis=0)
        charge[at] = jnp.concatenate(halves(jnp.where(half_values, tile_values, turned_values)), axis=0)
        charge[at + 1] = jnp.concatenate(halves(jnp.where(half_values, turned_values, tile_values)), axis=0)


def build_targets(coords, centre, targets, leaf):
    high, mid, low, norm_high, norm_mid, norm_low = pieces_of(coords, centre)
    one = jnp.ones_like(norm_high)
    rows = jnp.concatenate(
        [
            -2.0 * high, -2.0 * mid, one, one, -2.0 * low, -2.0 * high, one, norm_high,
            -2.0 * mid, -2.0 * high, norm_mid, norm_low, jnp.zeros((8, COL), F32),
        ],
        axis=0,
    )
    for pair in range(BZ // 2):
        tile = rows[:, pair * 128 : pair * 128 + 128].T.astype(BF16)
        targets[leaf + 2 * pair] = tile[:LEAF]
        targets[leaf + 2 * pair + 1] = tile[LEAF:]


def centre_of():
    top, leaf = lax.axis_index("top"), lax.axis_index("leaf")
    row = lax.broadcasted_iota(jnp.int32, (3, COL), 0)
    return jnp.where(row == 0, top.astype(F32) + 0.5, jnp.where(row == 1, leaf.astype(F32) + 0.5, 1.0))


def region(array, columns, first, count, to, centre, sources, charge):
    together = 4 if count % 4 == 0 else 2

    def step(index, carry):
        for part in range(together):
            i = together * index + part
            coords = coords_at(array, columns, first + i, part % 2)
            build_column(coords, array[:, column(first + i)], centre, to(i), sources, charge)
        return carry

    lax.fori_loop(0, count // together, step, 0)


def own_columns(coords, values, to, centre, sources, charge):
    def step(index, carry):
        for part in range(4):
            i = 4 * index + part
            at = column(i)
            build_column(coords[:, at], values[:, at], centre, to(i), sources, charge)
        return carry

    lax.fori_loop(0, COLS // 4, step, 0)


def gathered(array, ids, slot, target):
    half = low_lanes(32)
    four = [array[ids[slot + k, target]] for k in range(4)]
    return jnp.concatenate([jnp.where(half, four[0], four[1]), jnp.where(half, four[2], four[3])], axis=1)


def entries_of(square):
    square = jnp.maximum(square, 1e-20)
    scaled = square * lax.rsqrt(square)
    decay = jnp.exp2(scaled * -LOG2E)
    return jnp.concatenate(halves(decay + scaled * decay), axis=0)


def list_steps(steps, units, choose, ids, sources, charge, targets, squares, add):
    def distances(step, unit):
        target, slot = choose(step, unit)
        squares[unit] = dot(targets[target], gathered(sources, ids, slot, target))

    for unit in range(units):
        distances(0, unit)

    def run(step, carry):
        waiting = None
        for unit in range(units + 1):
            if unit < units:
                entries = entries_of(squares[unit])
                distances(jnp.minimum(step + 1, steps - 1), unit)
            if waiting is not None:
                target, slot = choose(step, unit - 1)
                product = dot(gathered(charge, ids, slot, target), waiting, NT)
                add(step, unit - 1, target, product[:RHS] + product[RHS:])
            waiting = entries
        return carry

    lax.fori_loop(0, steps, run, 0)


def near_pass(phase, cells, near_ids, work, points, centre, sources, charge, targets, squares, sums):
    for x, y in cells:
        col = x * BY + y
        build_targets(points[:, col * COL : col * COL + COL], centre, targets, col * BZ)

        def zero(i, carry, first=col * BZ):
            sums[first + i] = jnp.zeros((RHS, 128), F32)
            return carry

        lax.fori_loop(0, BZ, zero, 0)
    sources[NEAR_NULL] = jnp.zeros((32, 128), BF16)
    charge[NEAR_NULL] = jnp.zeros((32, 128), BF16)

    def choose(step, unit):
        code = work[phase, step * UNITS + unit]
        return code >> 3, (code & 7) * 4

    def add(step, unit, target, value):
        sums[target] = sums[target] + value

    steps = jnp.maximum((work[4 + phase, 0] + UNITS - 1) // UNITS, 1)
    list_steps(steps, UNITS, choose, near_ids, sources, charge, targets, squares, add)


def folded(sums, pair):
    first, second = sums[2 * pair], sums[2 * pair + 1]
    first = first + pltpu.roll(first, LEAF, 1)
    second = second + pltpu.roll(second, LEAF, 1)
    return jnp.where(low_lanes(RHS), first, second)


def near_store(cells, out, places, sums, charges):
    for (x, y), to in zip(cells, places):
        for pair in range(BZ // 2):
            at = (x * BY + y) * COL + pair * 128
            value = folded(sums, (x * BY + y) * (BZ // 2) + pair)
            out[:, to * COL + pair * 128 : to * COL + pair * 128 + 128] = value + NUGGET * charges[:, at : at + 128]


def near_own(points, charges, centre, sources, charge):
    own_columns(points, charges, lambda i: (i // BY + 1) * NX + i % BY + 1, centre, sources, charge)


def near_sides(from_down, from_up, centre, sources, charge):
    region(from_down, YCOLS, YFAR, YNEAR, lambda i: (i + 1) * NX, centre, sources, charge)
    region(from_up, YCOLS, YFAR, YNEAR, lambda i: (i + 1) * NX + NX - 1, centre, sources, charge)


def inner_kernel(near_ids, work, points, charges, out, sources, charge, targets, squares, sums):
    centre = centre_of()
    near_own(points, charges, centre, sources, charge)
    near_pass(0, INNER, near_ids, work, points, centre, sources, charge, targets, squares, sums)
    near_store(INNER, out, range(4), sums, charges)


def strip_kernel(
    near_ids, work, points, charges, skeleton, coef, from_down, from_up,
    out, far_sources, far_charge, far_targets,
    sources, charge, targets, squares, sums,
):
    centre = centre_of()
    near_own(points, charges, centre, sources, charge)
    near_sides(from_down, from_up, centre, sources, charge)
    near_pass(1, STRIP, near_ids, work, points, centre, sources, charge, targets, squares, sums)
    near_store(STRIP, out, range(4), sums, charges)
    own_columns(skeleton, coef, lambda i: i, centre, far_sources, far_charge)
    region(from_down, YCOLS, 0, YFAR, lambda i: COLS + i, centre, far_sources, far_charge)
    region(from_up, YCOLS, 0, YFAR, lambda i: COLS + YFAR + i, centre, far_sources, far_charge)

    def target_step(i, carry):
        for part in range(2):
            col = 2 * i + part
            build_targets(skeleton[:, column(col)], centre, far_targets, col * BZ)
        return carry

    lax.fori_loop(0, COLS // 2, target_step, 0)


def rest_kernel(
    near_ids, work, far_ids, points, charges, from_down, from_up, from_left, from_right,
    inner, strip, early_sources, early_charge, far_targets, near_out, far_out,
    sources, charge, targets, far_sources, far_charge, squares, sums,
):
    centre = centre_of()
    near_own(points, charges, centre, sources, charge)
    near_sides(from_down, from_up, centre, sources, charge)
    region(from_left, XCOLS, XFAR, XNEAR, lambda i: i, centre, sources, charge)
    region(from_right, XCOLS, XFAR, XNEAR, lambda i: (NX - 1) * NX + i, centre, sources, charge)
    near_pass(2, RIM, near_ids, work, points, centre, sources, charge, targets, squares, sums)
    near_store(RIM, near_out, [x * BY + y for x, y in RIM], sums, charges)
    for cells, done in ((INNER, inner), (STRIP, strip)):
        for i, (x, y) in enumerate(cells):
            near_out[:, column(x * BY + y)] = done[:, i * COL : i * COL + COL]

    def place(first, count, to):
        def step(i, carry):
            for leaf in range(BZ):
                at, source = to(i) * BZ + leaf, (first + i) * BZ + leaf
                far_sources[at] = early_sources[source]
                far_charge[at] = early_charge[source]
            return carry

        lax.fori_loop(0, count, step, 0)

    place(0, COLS, lambda i: (i // BY + 2) * FX + i % BY + 2)
    place(COLS, YFAR, lambda i: (i // 2 + 2) * FX + i % 2)
    place(COLS + YFAR, YFAR, lambda i: (i // 2 + 2) * FX + i % 2 + BY + 2)
    region(from_left, XCOLS, 0, XFAR, lambda i: i, centre, far_sources, far_charge)
    region(from_right, XCOLS, 0, XFAR, lambda i: (BX + 2) * FX + i, centre, far_sources, far_charge)

    def choose(step, unit):
        return step * 16 + unit // 4, unit % 4 * 4

    def add(step, unit, target, value):
        sums[target] = value if unit % 4 == 0 else sums[target] + value

    list_steps(HERE * 4 // 64, 64, choose, far_ids, far_sources, far_charge, far_targets, squares, add)

    def far_store(i, carry):
        far_out[:, pl.ds(pl.multiple_of(i * 128, 128), 128)] = folded(sums, i)
        return carry

    lax.fori_loop(0, HERE // 2, far_store, 0)


def last_kernel(
    device_far, rows, device_skeleton, branch_skeleton, branch_transfer, transfer, basis, near, far, out, coupling
):
    @pl.when(pl.program_id(0) == 0)
    def start():
        top, leaf = lax.axis_index("top"), lax.axis_index("leaf")
        same = lax.broadcasted_iota(jnp.int32, (LEAF, LEAF), 0) == lax.broadcasted_iota(
            jnp.int32, (LEAF, LEAF), 1
        )

        def upright(coords):
            return [
                jnp.sum(jnp.where(same, coords[i : i + 1], 0.0), axis=1, keepdims=True) for i in range(3)
            ]

        def kernel_block(own, other):
            total = 0.0
            for i in range(3):
                differ = own[i] - other[i : i + 1]
                total = total + differ * differ
            scaled = KERNEL_SCALE * jnp.sqrt(total)
            return SIGNAL * (1.0 + scaled) * jnp.exp(-scaled)

        def exact(a, b, dims):
            return lax.dot_general(a, b, dims, precision=EXACT, preferred_element_type=F32)

        def cluster(skeletons, index):
            tile = skeletons[:, pl.ds(pl.multiple_of(index // 2 * 128, 128), 128)]
            return jnp.where(index % 2 == 0, tile, pltpu.roll(tile, LEAF, 1))[:, :LEAF]

        own = upright(cluster(device_skeleton, top * 16 + leaf))
        coupled = jnp.zeros((RHS, LEAF), F32)
        for k in range(4):
            partner = jnp.minimum(jnp.maximum(device_far[k, 0], 0), 127)
            coupled = coupled + exact(rows[partner][:, :LEAF], kernel_block(own, cluster(device_skeleton, partner)), NT)
        own = upright(cluster(branch_skeleton, top))
        field = jnp.zeros((RHS, LEAF), F32)
        for e in range(8):
            total = rows[16 * e]
            for d in range(1, 16):
                total = total + rows[16 * e + d]
            weight = jnp.where(jnp.abs(e - top) >= 2, 1.0, 0.0)
            field = field + exact(total[:, LEAF:] * weight, kernel_block(own, cluster(branch_skeleton, e)), NT)
        coupled = coupled + exact(field, branch_transfer[...], NN)
        coupling[...] = coupled

    lifted = jnp.concatenate(halves(coupling[...]), axis=0)
    half = low_lanes(RHS)
    together = BLOCK // 256

    places, fields = [], []
    for part in range(together):
        place = slice(part * 256, part * 256 + 256)
        t_high, t_low = halves(transfer[:, place])
        up = dot(lifted, t_high) + dot(lifted, t_low)
        places.append(place)
        fields.append(far[:, place] + (up[:RHS] + up[RHS:]))
    products = []
    for place, value in zip(places, fields):
        pieces = []
        for i in range(4):
            tile = value[:, (i // 2) * 128 : (i // 2) * 128 + 128]
            tile = jnp.where(half, tile, 0.0) if i % 2 == 0 else jnp.where(half, 0.0, tile)
            pieces.extend(halves(tile))
        lines = jnp.concatenate(pieces, axis=0)
        b_high, b_low = halves(basis[:, place])
        products.append(
            dot(lines, jnp.concatenate([b_high, b_high], axis=0))
            + dot(lines, jnp.concatenate([b_low, b_low], axis=0))
        )
    for place, product in zip(places, products):
        each = [product[32 * i : 32 * i + 16] + product[32 * i + 16 : 32 * i + 32] for i in range(4)]
        result = jnp.concatenate(
            [
                jnp.where(half, each[0][:, :128], each[1][:, :128]),
                jnp.where(half, each[2][:, 128:], each[3][:, 128:]),
            ],
            axis=1,
        )
        out[:, place] = near[:, place] + result


def block(rows):
    return pl.BlockSpec((rows, BLOCK), lambda i: (0, i))


def shape(*dims, dtype=F32):
    return jax.ShapeDtypeStruct(dims, dtype)


def body(
    points,
    charges,
    near_list,
    far_list,
    leaf_basis,
    transfer,
    leaf_skeleton,
    device_far,
    branch_transfer,
    device_skeleton,
    branch_skeleton,
):
    here = charges.shape[1]

    def moved(array, axis, up):
        size = lax.axis_size(axis)
        pairs = [(i, i + 1) for i in range(size - 1)]
        return lax.ppermute(array, axis, pairs if up else [(j, i) for i, j in pairs])

    coef, device_row, near_ids, far_ids, work, send_down, send_up = pl.pallas_call(
        first_kernel,
        grid=(here // BLOCK,),
        in_specs=[VMEM] * 4 + [block(RANK)] * 2 + [VMEM] * 2,
        out_specs=[VMEM] * 7,
        scratch_shapes=[pltpu.VMEM((2 * RHS, LEAF), F32)],
        out_shape=[
            shape(RHS, here), shape(RHS, 128), shape(32, HERE, dtype=jnp.int32), shape(FAR, HERE, dtype=jnp.int32),
            shape(8, 512, dtype=jnp.int32), shape(RHS, YLANES), shape(RHS, YLANES),
        ],
        compiler_params=room(60),
        name="coefficients",
    )(points, charges, near_list, far_list, leaf_basis, transfer, leaf_skeleton, branch_transfer)
    every_row = lax.all_gather(device_row, ("top", "leaf"), axis=0)
    from_down = moved(send_up, "leaf", True)
    from_up = moved(send_down, "leaf", False)

    def scratch(leaves):
        return [
            pltpu.VMEM((leaves, 32, 128), BF16),
            pltpu.VMEM((leaves, 32, 128), BF16),
            pltpu.VMEM((HERE, LEAF, 32), BF16),
        ]

    common = [pltpu.VMEM((64, LEAF, 4 * LEAF), F32), pltpu.VMEM((HERE, RHS, 128), F32)]

    def cost(us):
        return pl.CostEstimate(flops=us * 10**9, bytes_accessed=10**6, transcendentals=0)

    inner = pl.pallas_call(
        inner_kernel,
        in_specs=[SMEM] * 2 + [VMEM] * 2,
        out_specs=VMEM,
        out_shape=shape(RHS, 4 * COL),
        scratch_shapes=scratch(NEAR_NULL + 1) + common,
        compiler_params=room(16),
        cost_estimate=cost(13),
        name="inner",
    )(near_ids, work, points, charges)
    send_left, send_right = pl.pallas_call(
        side_kernel,
        in_specs=[VMEM] * 6,
        out_specs=[VMEM] * 2,
        out_shape=[shape(RHS, XLANES), shape(RHS, XLANES)],
        compiler_params=room(12),
        name="sides",
    )(points, charges, leaf_skeleton, coef, from_down, from_up)
    from_left = moved(send_right, "top", True)
    from_right = moved(send_left, "top", False)
    early = (COLS + 2 * YFAR) * BZ
    strip, early_sources, early_charge, far_targets = pl.pallas_call(
        strip_kernel,
        in_specs=[SMEM] * 2 + [VMEM] * 6,
        out_specs=[VMEM] * 4,
        out_shape=[
            shape(RHS, 4 * COL), shape(early, 32, 128, dtype=BF16), shape(early, 32, 128, dtype=BF16),
            shape(HERE, LEAF, 32, dtype=BF16),
        ],
        scratch_shapes=scratch(NEAR_NULL + 1) + common,
        compiler_params=room(26),
        cost_estimate=cost(15),
        name="strip",
    )(near_ids, work, points, charges, leaf_skeleton, coef, from_down, from_up)
    near, far = pl.pallas_call(
        rest_kernel,
        in_specs=[SMEM] * 3 + [VMEM] * 11,
        out_specs=[VMEM] * 2,
        out_shape=[shape(RHS, here), shape(RHS, here)],
        scratch_shapes=scratch(NEAR_NULL + 1) + scratch(FAR_ALL)[:2] + common,
        compiler_params=room(34),
        cost_estimate=cost(55),
        name="rest",
    )(
        near_ids, work, far_ids, points, charges, from_down, from_up, from_left, from_right,
        inner, strip, early_sources, early_charge, far_targets,
    )
    return pl.pallas_call(
        last_kernel,
        grid=(here // BLOCK,),
        in_specs=[SMEM] + [VMEM] * 4 + [block(RANK)] * 2 + [block(RHS)] * 2,
        out_specs=block(RHS),
        scratch_shapes=[pltpu.VMEM((RHS, LEAF), F32)],
        out_shape=shape(RHS, here),
        compiler_params=room(60),
        name="fields",
    )(
        device_far,
        every_row,
        device_skeleton,
        branch_skeleton,
        branch_transfer,
        transfer,
        leaf_basis,
        near,
        far,
    )


def solution(mesh):
    split = P(None, ("top", "leaf"))
    return jax.shard_map(
        body, mesh=mesh, in_specs=(split,) * 9 + (P(), P()), out_specs=split, check_vma=False
    )
```

```python
import jax
import jax.numpy as jnp
from jax import lax
from jax.experimental import pallas as pl
from jax.experimental.pallas import tpu as pltpu
from jax.sharding import PartitionSpec as P

LEAF = 64
RANK = 64
RHS = 16
BX = 4
BY = 4
BZ = 8
COLS = BX * BY
COL = BZ * LEAF
HERE = COLS * BZ
NEAR = 27
FAR = 16
FAR_ROW, WORK_ROW, COUNT_ROW = 32, 48, 60
NX = BX + 2
FX = BX + 4
NEAR_NULL = NX * NX * BZ
FAR_ALL = FX * FX * BZ
YFAR, YNEAR = 2 * BX, BX
XFAR, XNEAR = 2 * FX, NX
YCOLS = YFAR + YNEAR
XCOLS = XFAR + XNEAR
YLANES = (YCOLS + (YCOLS + 3) // 4) * COL
XLANES = (XCOLS + (XCOLS + 3) // 4) * COL
UNITS = 32
BLOCK = 4096
INNER = ((1, 1), (1, 2), (2, 1), (2, 2))
STRIP = ((1, 0), (1, 3), (2, 0), (2, 3))
RIM = tuple((x, y) for x in (0, 3) for y in range(4))

EXACT = lax.Precision.HIGHEST
KERNEL_SCALE = 3.4641016151377544
LOG2E = 1.4426950408889634
SIGNAL = 0.0625
NUGGET = 0.25
BF16 = jnp.bfloat16
F32 = jnp.float32
NT = (((1,), (1,)), ((), ()))
NN = (((1,), (0,)), ((), ()))
VMEM = pl.BlockSpec(memory_space=pltpu.VMEM)
SMEM = pl.BlockSpec(memory_space=pltpu.SMEM)


def room(mib):
    return pltpu.CompilerParams(vmem_limit_bytes=mib * 2**20)


def dot(a, b, dims=NN):
    return lax.dot_general(a, b, dims, preferred_element_type=F32)


def halves(value):
    high = value.astype(BF16)
    return high, (value - high.astype(F32)).astype(BF16)


def low_lanes(rows):
    return lax.broadcasted_iota(jnp.int32, (rows, 128), 1) < LEAF


def column(index):
    return pl.ds(pl.multiple_of(index * COL, COL), COL)


def coords_at(array, columns, index, odd):
    row = pl.ds(pl.multiple_of(index // 2 % 2 * 8, 8), 8)
    return array[row, column(columns + index // 4)][3 * odd : 3 * odd + 3]


def set_coords(array, columns, index, value):
    row = index // 2 % 2 * 8 + index % 2 * 3
    array[row : row + 3, column(columns + index // 4)] = value


def window_ids(ids, width, span, top, leaf, null):
    wx = ((ids >> 11) - top) * BX + ((ids >> 5) & 3) + width
    wy = (((ids >> 7) & 15) - leaf) * BY + ((ids >> 3) & 3) + width
    place = (wx * span + wy) * BZ + (ids & 7)
    place = jnp.minimum(jnp.maximum(place, 0), span * span * BZ - 1)
    return jnp.where(ids >= 0, place, null)


def work_lists(used, table):
    lane = lax.broadcasted_iota(jnp.int32, (1, HERE), 1)
    inner_x = (((lane >> 5) + 1) & 2) != 0
    inner_y = ((((lane >> 3) & 3) + 1) & 2) != 0
    member = jnp.where(inner_x, jnp.where(inner_y, 0, 1), 2)
    parts = (used + 3) >> 2
    first = lax.broadcasted_iota(jnp.int32, (HERE, HERE), 0)
    second = lax.broadcasted_iota(jnp.int32, (HERE, HERE), 1)
    place = lax.broadcasted_iota(jnp.int32, (HERE, 512), 1)
    for phase in range(3):
        kept = jnp.where(member == phase, parts, 0)
        end = jnp.sum(jnp.where(second <= first, kept, 0), axis=1, keepdims=True)
        count = jnp.sum(jnp.where(second == first, kept, 0), axis=1, keepdims=True)
        passed = end <= place
        leaf = jnp.sum(jnp.where(passed, 1, 0), axis=0, keepdims=True)
        start = jnp.sum(jnp.where(passed, count, 0), axis=0, keepdims=True)
        code = leaf * 8 + (place[:1] - start)
        code = jnp.where(leaf < HERE, code, 7)
        for part in range(4):
            row = WORK_ROW + 4 * phase + part
            table[row : row + 1] = code[:, part * 128 : part * 128 + 128]
        row = COUNT_ROW + phase
        table[row : row + 1] = jnp.zeros((1, 128), jnp.int32) + jnp.sum(kept, axis=1, keepdims=True)


def first_kernel(
    points, charges, near_list, far_list, basis, transfer, skeleton, branch_transfer,
    coef, device_row, table, send_down, send_up, total,
):
    lane = lax.broadcasted_iota(jnp.int32, (2 * RHS, 4 * LEAF), 1) // LEAF
    half = low_lanes(RHS)
    together = BLOCK // 256
    index = pl.program_id(0)

    places, products = [], []
    for part in range(together):
        place = pl.ds(pl.multiple_of(index * BLOCK + part * 256, 256), 256)
        here = slice(part * 256, part * 256 + 256)
        places.append((place, here))
        q_high, q_low = halves(charges[:, place])
        q = jnp.concatenate([q_high, q_low], axis=0)
        zero = jnp.zeros_like(q)
        rows = jnp.concatenate([jnp.where(lane == i, q, zero) for i in range(4)], axis=0)
        b_high, b_low = halves(basis[:, here])
        products.append(
            dot(rows, jnp.concatenate([b_high, b_high], axis=0), NT)
            + dot(rows, jnp.concatenate([b_low, b_low], axis=0), NT)
        )
    sums = []
    for (place, here), product in zip(places, products):
        each = [product[32 * i : 32 * i + 16] + product[32 * i + 16 : 32 * i + 32] for i in range(4)]
        value = jnp.concatenate(
            [jnp.where(half, each[0], each[1]), jnp.where(half, each[2], each[3])], axis=1
        )
        coef[:, place] = value
        c = jnp.concatenate(halves(value), axis=0)
        t_high, t_low = halves(transfer[:, here])
        sums.append(dot(c, t_high, NT) + dot(c, t_low, NT))

    @pl.when(index == 0)
    def start():
        total[...] = jnp.zeros((2 * RHS, LEAF), F32)

    total[...] = total[...] + sum(sums[1:], sums[0])

    @pl.when(index == HERE * LEAF // BLOCK - 1)
    def finish():
        top, leaf = lax.axis_index("top"), lax.axis_index("leaf")
        listed = near_list[...]
        table[0:NEAR] = window_ids(listed, 1, NX, top, leaf, NEAR_NULL)
        table[NEAR:32] = jnp.full((5, HERE), NEAR_NULL, jnp.int32)
        table[COUNT_ROW:64] = jnp.zeros((64 - COUNT_ROW, HERE), jnp.int32)
        work_lists(jnp.sum((listed >= 0).astype(jnp.int32), axis=0, keepdims=True), table)
        table[FAR_ROW : FAR_ROW + FAR] = window_ids(far_list[...], 2, FX, top, leaf, 0)

        own = total[0:RHS] + total[RHS : 2 * RHS]
        raised = lax.dot_general(own, branch_transfer[...], NT, precision=EXACT, preferred_element_type=F32)
        device_row[...] = jnp.concatenate([own, raised], axis=1)

        def fill(target, near_y, far_y):
            for x in range(BX):
                for y in range(2):
                    at = column(x * BY + far_y + y)
                    target[:, column(x * 2 + y)] = coef[:, at]
                    set_coords(target, YCOLS, x * 2 + y, skeleton[:, at])
                at = column(x * BY + near_y)
                target[:, column(YFAR + x)] = charges[:, at]
                set_coords(target, YCOLS, YFAR + x, points[:, at])

        blank = jnp.zeros((RHS, YLANES - YCOLS * COL), F32)
        send_down[:, YCOLS * COL : YLANES] = blank
        send_up[:, YCOLS * COL : YLANES] = blank
        fill(send_down, 0, 0)
        fill(send_up, BY - 1, BY - 2)


def side_kernel(points, charges, skeleton, coef, from_down, from_up, send_left, send_right):
    def fill(target, near_x, far_x):
        def put(index, values, coords):
            target[:, column(index)] = values
            set_coords(target, XCOLS, index, coords)

        def side(index, array, at):
            put(index, array[:, column(at)], coords_at(array, YCOLS, at, at % 2))

        for x in range(2):
            at_x = far_x + x
            for y in range(2):
                side(x * FX + y, from_down, at_x * 2 + y)
                side(x * FX + y + BY + 2, from_up, at_x * 2 + y)
            for y in range(BY):
                at = column(at_x * BY + y)
                put(x * FX + 2 + y, coef[:, at], skeleton[:, at])
        side(XFAR, from_down, YFAR + near_x)
        side(XFAR + BY + 1, from_up, YFAR + near_x)
        for y in range(BY):
            at = column(near_x * BY + y)
            put(XFAR + 1 + y, charges[:, at], points[:, at])

    blank = jnp.zeros((RHS, XLANES - XCOLS * COL), F32)
    send_left[:, XCOLS * COL : XLANES] = blank
    send_right[:, XCOLS * COL : XLANES] = blank
    fill(send_left, 0, 0)
    fill(send_right, BX - 1, BX - 2)


def pieces_of(coords, centre):
    place = (coords - centre) * KERNEL_SCALE
    high = place.astype(BF16).astype(F32)
    rest = place - high
    mid = rest.astype(BF16).astype(F32)
    norm = jnp.sum(place * place, axis=0, keepdims=True)
    norm_high = norm.astype(BF16).astype(F32)
    norm_rest = norm - norm_high
    norm_mid = norm_rest.astype(BF16).astype(F32)
    return high, mid, rest - mid, norm_high, norm_mid, norm_rest - norm_mid


def build_column(coords, values, centre, col, sources, charge):
    high, mid, low, norm_high, norm_mid, norm_low = pieces_of(coords, centre)
    one = jnp.ones_like(norm_high)
    empty = jnp.zeros((8, 128), BF16)
    rows = jnp.concatenate([high, high, norm_high, norm_mid, high, mid, norm_low, one, mid, low, one, one], axis=0)
    half = low_lanes(24)
    half_values = low_lanes(RHS)
    scaled = values * SIGNAL
    for pair in range(BZ // 2):
        lanes = slice(pair * 128, pair * 128 + 128)
        tile, tile_values = rows[:, lanes], scaled[:, lanes]
        turned, turned_values = pltpu.roll(tile, LEAF, 1), pltpu.roll(tile_values, LEAF, 1)
        at = col * BZ + 2 * pair
        sources[at] = jnp.concatenate([jnp.where(half, tile, turned).astype(BF16), empty], axis=0)
        sources[at + 1] = jnp.concatenate([jnp.where(half, turned, tile).astype(BF16), empty], axis=0)
        charge[at] = jnp.concatenate(halves(jnp.where(half_values, tile_values, turned_values)), axis=0)
        charge[at + 1] = jnp.concatenate(halves(jnp.where(half_values, turned_values, tile_values)), axis=0)


def build_targets(coords, centre, targets, leaf):
    high, mid, low, norm_high, norm_mid, norm_low = pieces_of(coords, centre)
    one = jnp.ones_like(norm_high)
    rows = jnp.concatenate(
        [
            -2.0 * high, -2.0 * mid, one, one, -2.0 * low, -2.0 * high, one, norm_high,
            -2.0 * mid, -2.0 * high, norm_mid, norm_low, jnp.zeros((8, COL), F32),
        ],
        axis=0,
    )
    for pair in range(BZ // 2):
        tile = rows[:, pair * 128 : pair * 128 + 128].T.astype(BF16)
        targets[leaf + 2 * pair] = tile[:LEAF]
        targets[leaf + 2 * pair + 1] = tile[LEAF:]


def centre_of():
    top, leaf = lax.axis_index("top"), lax.axis_index("leaf")
    row = lax.broadcasted_iota(jnp.int32, (3, COL), 0)
    return jnp.where(row == 0, top.astype(F32) + 0.5, jnp.where(row == 1, leaf.astype(F32) + 0.5, 1.0))


def region(array, columns, first, count, to, centre, sources, charge):
    together = 4 if count % 4 == 0 else 2

    def step(index, carry):
        for part in range(together):
            i = together * index + part
            coords = coords_at(array, columns, first + i, part % 2)
            build_column(coords, array[:, column(first + i)], centre, to(i), sources, charge)
        return carry

    lax.fori_loop(0, count // together, step, 0)


def own_columns(coords, values, to, centre, sources, charge):
    def step(index, carry):
        for part in range(4):
            i = 4 * index + part
            at = column(i)
            build_column(coords[:, at], values[:, at], centre, to(i), sources, charge)
        return carry

    lax.fori_loop(0, COLS // 4, step, 0)


def gathered(array, ids, slot, target):
    half = low_lanes(32)
    four = [array[ids[slot + k, target]] for k in range(4)]
    return jnp.concatenate([jnp.where(half, four[0], four[1]), jnp.where(half, four[2], four[3])], axis=1)


def entries_of(square):
    square = jnp.maximum(square, 1e-20)
    scaled = square * lax.rsqrt(square)
    decay = jnp.exp2(scaled * -LOG2E)
    return jnp.concatenate(halves(decay + scaled * decay), axis=0)


def list_steps(steps, units, choose, ids, sources, charge, targets, squares, add):
    def distances(step, unit):
        target, slot = choose(step, unit)
        squares[unit] = dot(targets[target], gathered(sources, ids, slot, target))

    for unit in range(units):
        distances(0, unit)

    def run(step, carry):
        waiting = None
        for unit in range(units + 1):
            if unit < units:
                entries = entries_of(squares[unit])
                distances(jnp.minimum(step + 1, steps - 1), unit)
            if waiting is not None:
                target, slot = choose(step, unit - 1)
                product = dot(gathered(charge, ids, slot, target), waiting, NT)
                add(step, unit - 1, target, product[:RHS] + product[RHS:])
            waiting = entries
        return carry

    lax.fori_loop(0, steps, run, 0)


def near_pass(phase, cells, table, points, centre, sources, charge, targets, squares, sums):
    for x, y in cells:
        col = x * BY + y
        build_targets(points[:, col * COL : col * COL + COL], centre, targets, col * BZ)

        def zero(i, carry, first=col * BZ):
            sums[first + i] = jnp.zeros((RHS, 128), F32)
            return carry

        lax.fori_loop(0, BZ, zero, 0)
    sources[NEAR_NULL] = jnp.zeros((32, 128), BF16)
    charge[NEAR_NULL] = jnp.zeros((32, 128), BF16)

    def choose(step, unit):
        place = step * UNITS + unit
        code = table[WORK_ROW + 4 * phase + (place >> 7), place & 127]
        return code >> 3, (code & 7) * 4

    def add(step, unit, target, value):
        sums[target] = sums[target] + value

    steps = jnp.maximum((table[COUNT_ROW + phase, 0] + UNITS - 1) // UNITS, 1)
    list_steps(steps, UNITS, choose, table, sources, charge, targets, squares, add)


def folded(sums, pair):
    first, second = sums[2 * pair], sums[2 * pair + 1]
    first = first + pltpu.roll(first, LEAF, 1)
    second = second + pltpu.roll(second, LEAF, 1)
    return jnp.where(low_lanes(RHS), first, second)


def near_store(cells, out, places, sums, charges):
    for (x, y), to in zip(cells, places):
        for pair in range(BZ // 2):
            at = (x * BY + y) * COL + pair * 128
            value = folded(sums, (x * BY + y) * (BZ // 2) + pair)
            out[:, to * COL + pair * 128 : to * COL + pair * 128 + 128] = value + NUGGET * charges[:, at : at + 128]


def near_own(points, charges, centre, sources, charge):
    own_columns(points, charges, lambda i: (i // BY + 1) * NX + i % BY + 1, centre, sources, charge)


def near_sides(from_down, from_up, centre, sources, charge):
    region(from_down, YCOLS, YFAR, YNEAR, lambda i: (i + 1) * NX, centre, sources, charge)
    region(from_up, YCOLS, YFAR, YNEAR, lambda i: (i + 1) * NX + NX - 1, centre, sources, charge)


def inner_kernel(table, points, charges, out, sources, charge, targets, squares, sums):
    centre = centre_of()
    near_own(points, charges, centre, sources, charge)
    near_pass(0, INNER, table, points, centre, sources, charge, targets, squares, sums)
    near_store(INNER, out, range(4), sums, charges)


def strip_kernel(
    table, points, charges, skeleton, coef, from_down, from_up,
    out, far_sources, far_charge, far_targets, sources, charge,
    targets, squares, sums,
):
    centre = centre_of()
    near_own(points, charges, centre, sources, charge)
    near_sides(from_down, from_up, centre, sources, charge)
    near_pass(1, STRIP, table, points, centre, sources, charge, targets, squares, sums)
    near_store(STRIP, out, range(4), sums, charges)
    own_columns(skeleton, coef, lambda i: i, centre, far_sources, far_charge)
    region(from_down, YCOLS, 0, YFAR, lambda i: COLS + i, centre, far_sources, far_charge)
    region(from_up, YCOLS, 0, YFAR, lambda i: COLS + YFAR + i, centre, far_sources, far_charge)

    def target_step(i, carry):
        for part in range(2):
            col = 2 * i + part
            build_targets(skeleton[:, column(col)], centre, far_targets, col * BZ)
        return carry

    lax.fori_loop(0, COLS // 2, target_step, 0)


def rest_kernel(
    table, points, charges, from_down, from_up, from_left, from_right,
    inner, strip, early_sources, early_charge, far_targets, near_sources, near_charge, near_out, far_out,
    sources, charge, targets, far_sources, far_charge, squares, sums,
):
    centre = centre_of()
    def keep(i, carry):
        for leaf in range(BZ):
            at = NX * BZ + i * BZ + leaf
            sources[at] = near_sources[at]
            charge[at] = near_charge[at]
        return carry

    lax.fori_loop(0, BX * NX, keep, 0)
    region(from_left, XCOLS, XFAR, XNEAR, lambda i: i, centre, sources, charge)
    region(from_right, XCOLS, XFAR, XNEAR, lambda i: (NX - 1) * NX + i, centre, sources, charge)
    near_pass(2, RIM, table, points, centre, sources, charge, targets, squares, sums)
    near_store(RIM, near_out, [x * BY + y for x, y in RIM], sums, charges)
    for cells, done in ((INNER, inner), (STRIP, strip)):
        for i, (x, y) in enumerate(cells):
            near_out[:, column(x * BY + y)] = done[:, i * COL : i * COL + COL]

    def place(first, count, to):
        def step(i, carry):
            for leaf in range(BZ):
                at, source = to(i) * BZ + leaf, (first + i) * BZ + leaf
                far_sources[at] = early_sources[source]
                far_charge[at] = early_charge[source]
            return carry

        lax.fori_loop(0, count, step, 0)

    place(0, COLS, lambda i: (i // BY + 2) * FX + i % BY + 2)
    place(COLS, YFAR, lambda i: (i // 2 + 2) * FX + i % 2)
    place(COLS + YFAR, YFAR, lambda i: (i // 2 + 2) * FX + i % 2 + BY + 2)
    region(from_left, XCOLS, 0, XFAR, lambda i: i, centre, far_sources, far_charge)
    region(from_right, XCOLS, 0, XFAR, lambda i: (BX + 2) * FX + i, centre, far_sources, far_charge)

    def choose(step, unit):
        return step * 16 + unit // 4, FAR_ROW + unit % 4 * 4

    def add(step, unit, target, value):
        sums[target] = value if unit % 4 == 0 else sums[target] + value

    list_steps(HERE * 4 // 64, 64, choose, table, far_sources, far_charge, far_targets, squares, add)

    def far_store(i, carry):
        far_out[:, pl.ds(pl.multiple_of(i * 128, 128), 128)] = folded(sums, i)
        return carry

    lax.fori_loop(0, HERE // 2, far_store, 0)


def last_kernel(
    device_far, rows, device_skeleton, branch_skeleton, branch_transfer, transfer, basis, near, far, out, coupling
):
    @pl.when(pl.program_id(0) == 0)
    def start():
        top, leaf = lax.axis_index("top"), lax.axis_index("leaf")
        same = lax.broadcasted_iota(jnp.int32, (LEAF, LEAF), 0) == lax.broadcasted_iota(
            jnp.int32, (LEAF, LEAF), 1
        )

        def upright(coords):
            return [
                jnp.sum(jnp.where(same, coords[i : i + 1], 0.0), axis=1, keepdims=True) for i in range(3)
            ]

        def kernel_block(own, other):
            total = 0.0
            for i in range(3):
                differ = own[i] - other[i : i + 1]
                total = total + differ * differ
            scaled = KERNEL_SCALE * jnp.sqrt(total)
            return SIGNAL * (1.0 + scaled) * jnp.exp(-scaled)

        def exact(a, b, dims):
            return lax.dot_general(a, b, dims, precision=EXACT, preferred_element_type=F32)

        def cluster(skeletons, index):
            tile = skeletons[:, pl.ds(pl.multiple_of(index // 2 * 128, 128), 128)]
            return jnp.where(index % 2 == 0, tile, pltpu.roll(tile, LEAF, 1))[:, :LEAF]

        own = upright(cluster(device_skeleton, top * 16 + leaf))
        coupled = jnp.zeros((RHS, LEAF), F32)
        for k in range(4):
            partner = jnp.minimum(jnp.maximum(device_far[k, 0], 0), 127)
            coupled = coupled + exact(rows[partner][:, :LEAF], kernel_block(own, cluster(device_skeleton, partner)), NT)
        own = upright(cluster(branch_skeleton, top))
        field = jnp.zeros((RHS, LEAF), F32)
        for e in range(8):
            total = rows[16 * e]
            for d in range(1, 16):
                total = total + rows[16 * e + d]
            weight = jnp.where(jnp.abs(e - top) >= 2, 1.0, 0.0)
            field = field + exact(total[:, LEAF:] * weight, kernel_block(own, cluster(branch_skeleton, e)), NT)
        coupled = coupled + exact(field, branch_transfer[...], NN)
        coupling[...] = coupled

    lifted = jnp.concatenate(halves(coupling[...]), axis=0)
    half = low_lanes(RHS)
    together = BLOCK // 256

    places, fields = [], []
    for part in range(together):
        place = slice(part * 256, part * 256 + 256)
        t_high, t_low = halves(transfer[:, place])
        up = dot(lifted, t_high) + dot(lifted, t_low)
        places.append(place)
        fields.append(far[:, place] + (up[:RHS] + up[RHS:]))
    products = []
    for place, value in zip(places, fields):
        pieces = []
        for i in range(4):
            tile = value[:, (i // 2) * 128 : (i // 2) * 128 + 128]
            tile = jnp.where(half, tile, 0.0) if i % 2 == 0 else jnp.where(half, 0.0, tile)
            pieces.extend(halves(tile))
        lines = jnp.concatenate(pieces, axis=0)
        b_high, b_low = halves(basis[:, place])
        products.append(
            dot(lines, jnp.concatenate([b_high, b_high], axis=0))
            + dot(lines, jnp.concatenate([b_low, b_low], axis=0))
        )
    for place, product in zip(places, products):
        each = [product[32 * i : 32 * i + 16] + product[32 * i + 16 : 32 * i + 32] for i in range(4)]
        result = jnp.concatenate(
            [
                jnp.where(half, each[0][:, :128], each[1][:, :128]),
                jnp.where(half, each[2][:, 128:], each[3][:, 128:]),
            ],
            axis=1,
        )
        out[:, place] = near[:, place] + result


def block(rows):
    return pl.BlockSpec((rows, BLOCK), lambda i: (0, i))


def shape(*dims, dtype=F32):
    return jax.ShapeDtypeStruct(dims, dtype)


def body(
    points,
    charges,
    near_list,
    far_list,
    leaf_basis,
    transfer,
    leaf_skeleton,
    device_far,
    branch_transfer,
    device_skeleton,
    branch_skeleton,
):
    here = charges.shape[1]

    def moved(array, axis, up):
        size = lax.axis_size(axis)
        pairs = [(i, i + 1) for i in range(size - 1)]
        return lax.ppermute(array, axis, pairs if up else [(j, i) for i, j in pairs])

    coef, device_row, table, send_down, send_up = pl.pallas_call(
        first_kernel,
        grid=(here // BLOCK,),
        in_specs=[VMEM] * 4 + [block(RANK)] * 2 + [VMEM] * 2,
        out_specs=[VMEM] * 5,
        scratch_shapes=[pltpu.VMEM((2 * RHS, LEAF), F32)],
        out_shape=[
            shape(RHS, here), shape(RHS, 128), shape(64, HERE, dtype=jnp.int32), shape(RHS, YLANES), shape(RHS, YLANES),
        ],
        compiler_params=room(60),
        name="coefficients",
    )(points, charges, near_list, far_list, leaf_basis, transfer, leaf_skeleton, branch_transfer)
    every_row = lax.all_gather(device_row, ("top", "leaf"), axis=0)
    from_down = moved(send_up, "leaf", True)
    from_up = moved(send_down, "leaf", False)

    def scratch(leaves):
        return [
            pltpu.VMEM((leaves, 32, 128), BF16),
            pltpu.VMEM((leaves, 32, 128), BF16),
            pltpu.VMEM((HERE, LEAF, 32), BF16),
        ]

    common = [pltpu.VMEM((64, LEAF, 4 * LEAF), F32), pltpu.VMEM((HERE, RHS, 128), F32)]

    def cost(us):
        return pl.CostEstimate(flops=us * 10**9, bytes_accessed=10**6, transcendentals=0)

    inner = pl.pallas_call(
        inner_kernel,
        in_specs=[SMEM] + [VMEM] * 2,
        out_specs=VMEM,
        out_shape=shape(RHS, 4 * COL),
        scratch_shapes=scratch(NEAR_NULL + 1) + common,
        compiler_params=room(16),
        cost_estimate=cost(13),
        name="inner",
    )(table, points, charges)
    send_left, send_right = pl.pallas_call(
        side_kernel,
        in_specs=[VMEM] * 6,
        out_specs=[VMEM] * 2,
        out_shape=[shape(RHS, XLANES), shape(RHS, XLANES)],
        compiler_params=room(12),
        name="sides",
    )(points, charges, leaf_skeleton, coef, from_down, from_up)
    from_left = moved(send_right, "top", True)
    from_right = moved(send_left, "top", False)
    early = (COLS + 2 * YFAR) * BZ
    strip, early_sources, early_charge, far_targets, near_sources, near_charge = pl.pallas_call(
        strip_kernel,
        in_specs=[SMEM] + [VMEM] * 6,
        out_specs=[VMEM] * 6,
        out_shape=[
            shape(RHS, 4 * COL), shape(early, 32, 128, dtype=BF16), shape(early, 32, 128, dtype=BF16),
            shape(HERE, LEAF, 32, dtype=BF16), shape(NEAR_NULL + 1, 32, 128, dtype=BF16),
            shape(NEAR_NULL + 1, 32, 128, dtype=BF16),
        ],
        scratch_shapes=scratch(NEAR_NULL + 1)[2:] + common,
        compiler_params=room(28),
        cost_estimate=cost(15),
        name="strip",
    )(table, points, charges, leaf_skeleton, coef, from_down, from_up)
    near, far = pl.pallas_call(
        rest_kernel,
        in_specs=[SMEM] + [VMEM] * 13,
        out_specs=[VMEM] * 2,
        out_shape=[shape(RHS, here), shape(RHS, here)],
        scratch_shapes=scratch(NEAR_NULL + 1) + scratch(FAR_ALL)[:2] + common,
        compiler_params=room(38),
        cost_estimate=cost(55),
        name="rest",
    )(
        table, points, charges, from_down, from_up, from_left, from_right,
        inner, strip, early_sources, early_charge, far_targets, near_sources, near_charge,
    )
    return pl.pallas_call(
        last_kernel,
        grid=(here // BLOCK,),
        in_specs=[SMEM] + [VMEM] * 4 + [block(RANK)] * 2 + [block(RHS)] * 2,
        out_specs=block(RHS),
        scratch_shapes=[pltpu.VMEM((RHS, LEAF), F32)],
        out_shape=shape(RHS, here),
        compiler_params=room(60),
        name="fields",
    )(
        device_far,
        every_row,
        device_skeleton,
        branch_skeleton,
        branch_transfer,
        transfer,
        leaf_basis,
        near,
        far,
    )


def solution(mesh):
    split = P(None, ("top", "leaf"))
    return jax.shard_map(
        body, mesh=mesh, in_specs=(split,) * 9 + (P(), P()), out_specs=split, check_vma=False
    )
```

```python
import jax
import jax.numpy as jnp
from jax import lax
from jax.experimental import pallas as pl
from jax.experimental.pallas import tpu as pltpu
from jax.sharding import PartitionSpec as P

LEAF = 64
RANK = 64
RHS = 16
BX = 4
BY = 4
BZ = 8
COLS = BX * BY
COL = BZ * LEAF
HERE = COLS * BZ
NEAR = 27
FAR = 16
FAR_ROW, WORK_ROW, COUNT_ROW = 32, 48, 60
NX = BX + 2
FX = BX + 4
NEAR_NULL = NX * NX * BZ
FAR_ALL = FX * FX * BZ
YFAR, YNEAR = 2 * BX, BX
XFAR, XNEAR = 2 * FX, NX
YCOLS = YFAR + YNEAR
XCOLS = XFAR + XNEAR
YLANES = (YCOLS + (YCOLS + 3) // 4) * COL
XLANES = (XCOLS + (XCOLS + 3) // 4) * COL
UNITS = 32
BLOCK = 4096
INNER = ((1, 1), (1, 2), (2, 1), (2, 2))
STRIP = ((1, 0), (1, 3), (2, 0), (2, 3))
RIM = tuple((x, y) for x in (0, 3) for y in range(4))

EXACT = lax.Precision.HIGHEST
KERNEL_SCALE = 3.4641016151377544
LOG2E = 1.4426950408889634
SIGNAL = 0.0625
NUGGET = 0.25
BF16 = jnp.bfloat16
F32 = jnp.float32
NT = (((1,), (1,)), ((), ()))
NN = (((1,), (0,)), ((), ()))
VMEM = pl.BlockSpec(memory_space=pltpu.VMEM)
SMEM = pl.BlockSpec(memory_space=pltpu.SMEM)


def room(mib):
    return pltpu.CompilerParams(vmem_limit_bytes=mib * 2**20)


def dot(a, b, dims=NN):
    return lax.dot_general(a, b, dims, preferred_element_type=F32)


def halves(value):
    high = value.astype(BF16)
    return high, (value - high.astype(F32)).astype(BF16)


def low_lanes(rows):
    return lax.broadcasted_iota(jnp.int32, (rows, 128), 1) < LEAF


def column(index):
    return pl.ds(pl.multiple_of(index * COL, COL), COL)


def coords_at(array, columns, index, odd):
    row = pl.ds(pl.multiple_of(index // 2 % 2 * 8, 8), 8)
    return array[row, column(columns + index // 4)][3 * odd : 3 * odd + 3]


def set_coords(array, columns, index, value):
    row = index // 2 % 2 * 8 + index % 2 * 3
    array[row : row + 3, column(columns + index // 4)] = value


def window_ids(ids, width, span, top, leaf, null):
    wx = ((ids >> 11) - top) * BX + ((ids >> 5) & 3) + width
    wy = (((ids >> 7) & 15) - leaf) * BY + ((ids >> 3) & 3) + width
    place = (wx * span + wy) * BZ + (ids & 7)
    place = jnp.minimum(jnp.maximum(place, 0), span * span * BZ - 1)
    return jnp.where(ids >= 0, place, null)


def work_lists(used, table):
    lane = lax.broadcasted_iota(jnp.int32, (1, HERE), 1)
    inner_x = (((lane >> 5) + 1) & 2) != 0
    inner_y = ((((lane >> 3) & 3) + 1) & 2) != 0
    member = jnp.where(inner_x, jnp.where(inner_y, 0, 1), 2)
    parts = (used + 3) >> 2
    first = lax.broadcasted_iota(jnp.int32, (HERE, HERE), 0)
    second = lax.broadcasted_iota(jnp.int32, (HERE, HERE), 1)
    place = lax.broadcasted_iota(jnp.int32, (HERE, 512), 1)
    for phase in range(3):
        kept = jnp.where(member == phase, parts, 0)
        end = jnp.sum(jnp.where(second <= first, kept, 0), axis=1, keepdims=True)
        count = jnp.sum(jnp.where(second == first, kept, 0), axis=1, keepdims=True)
        passed = end <= place
        leaf = jnp.sum(jnp.where(passed, 1, 0), axis=0, keepdims=True)
        start = jnp.sum(jnp.where(passed, count, 0), axis=0, keepdims=True)
        code = leaf * 8 + (place[:1] - start)
        code = jnp.where(leaf < HERE, code, 7)
        for part in range(4):
            row = WORK_ROW + 4 * phase + part
            table[row : row + 1] = code[:, part * 128 : part * 128 + 128]
        row = COUNT_ROW + phase
        table[row : row + 1] = jnp.zeros((1, 128), jnp.int32) + jnp.sum(kept, axis=1, keepdims=True)


def first_kernel(
    points, charges, near_list, far_list, basis, transfer, skeleton, branch_transfer,
    coef, device_row, table, send_down, send_up, total,
):
    lane = lax.broadcasted_iota(jnp.int32, (2 * RHS, 4 * LEAF), 1) // LEAF
    half = low_lanes(RHS)
    together = BLOCK // 256
    index = pl.program_id(0)

    places, products = [], []
    for part in range(together):
        place = pl.ds(pl.multiple_of(index * BLOCK + part * 256, 256), 256)
        here = slice(part * 256, part * 256 + 256)
        places.append((place, here))
        q_high, q_low = halves(charges[:, place])
        q = jnp.concatenate([q_high, q_low], axis=0)
        zero = jnp.zeros_like(q)
        rows = jnp.concatenate([jnp.where(lane == i, q, zero) for i in range(4)], axis=0)
        b_high, b_low = halves(basis[:, here])
        products.append(
            dot(rows, jnp.concatenate([b_high, b_high], axis=0), NT)
            + dot(rows, jnp.concatenate([b_low, b_low], axis=0), NT)
        )
    sums = []
    for (place, here), product in zip(places, products):
        each = [product[32 * i : 32 * i + 16] + product[32 * i + 16 : 32 * i + 32] for i in range(4)]
        value = jnp.concatenate(
            [jnp.where(half, each[0], each[1]), jnp.where(half, each[2], each[3])], axis=1
        )
        coef[:, place] = value
        c = jnp.concatenate(halves(value), axis=0)
        t_high, t_low = halves(transfer[:, here])
        sums.append(dot(c, t_high, NT) + dot(c, t_low, NT))

    @pl.when(index == 0)
    def start():
        total[...] = jnp.zeros((2 * RHS, LEAF), F32)

    total[...] = total[...] + sum(sums[1:], sums[0])

    @pl.when(index == HERE * LEAF // BLOCK - 1)
    def finish():
        top, leaf = lax.axis_index("top"), lax.axis_index("leaf")
        listed = near_list[...]
        table[0:NEAR] = window_ids(listed, 1, NX, top, leaf, NEAR_NULL)
        table[NEAR:32] = jnp.full((5, HERE), NEAR_NULL, jnp.int32)
        table[COUNT_ROW:64] = jnp.zeros((64 - COUNT_ROW, HERE), jnp.int32)
        work_lists(jnp.sum((listed >= 0).astype(jnp.int32), axis=0, keepdims=True), table)
        table[FAR_ROW : FAR_ROW + FAR] = window_ids(far_list[...], 2, FX, top, leaf, 0)

        own = total[0:RHS] + total[RHS : 2 * RHS]
        raised = lax.dot_general(own, branch_transfer[...], NT, precision=EXACT, preferred_element_type=F32)
        device_row[...] = jnp.concatenate([own, raised], axis=1)

        def fill(target, near_y, far_y):
            for x in range(BX):
                for y in range(2):
                    at = column(x * BY + far_y + y)
                    target[:, column(x * 2 + y)] = coef[:, at]
                    set_coords(target, YCOLS, x * 2 + y, skeleton[:, at])
                at = column(x * BY + near_y)
                target[:, column(YFAR + x)] = charges[:, at]
                set_coords(target, YCOLS, YFAR + x, points[:, at])

        blank = jnp.zeros((RHS, YLANES - YCOLS * COL), F32)
        send_down[:, YCOLS * COL : YLANES] = blank
        send_up[:, YCOLS * COL : YLANES] = blank
        fill(send_down, 0, 0)
        fill(send_up, BY - 1, BY - 2)


def side_kernel(points, charges, skeleton, coef, from_down, from_up, send_left, send_right):
    def fill(target, near_x, far_x):
        def put(index, values, coords):
            target[:, column(index)] = values
            set_coords(target, XCOLS, index, coords)

        def side(index, array, at):
            put(index, array[:, column(at)], coords_at(array, YCOLS, at, at % 2))

        for x in range(2):
            at_x = far_x + x
            for y in range(2):
                side(x * FX + y, from_down, at_x * 2 + y)
                side(x * FX + y + BY + 2, from_up, at_x * 2 + y)
            for y in range(BY):
                at = column(at_x * BY + y)
                put(x * FX + 2 + y, coef[:, at], skeleton[:, at])
        side(XFAR, from_down, YFAR + near_x)
        side(XFAR + BY + 1, from_up, YFAR + near_x)
        for y in range(BY):
            at = column(near_x * BY + y)
            put(XFAR + 1 + y, charges[:, at], points[:, at])

    blank = jnp.zeros((RHS, XLANES - XCOLS * COL), F32)
    send_left[:, XCOLS * COL : XLANES] = blank
    send_right[:, XCOLS * COL : XLANES] = blank
    fill(send_left, 0, 0)
    fill(send_right, BX - 1, BX - 2)


def pieces_of(coords, centre):
    place = (coords - centre) * KERNEL_SCALE
    high = place.astype(BF16).astype(F32)
    rest = place - high
    mid = rest.astype(BF16).astype(F32)
    norm = jnp.sum(place * place, axis=0, keepdims=True)
    norm_high = norm.astype(BF16).astype(F32)
    norm_rest = norm - norm_high
    norm_mid = norm_rest.astype(BF16).astype(F32)
    return high, mid, rest - mid, norm_high, norm_mid, norm_rest - norm_mid


def build_column(coords, values, centre, col, sources, charge):
    high, mid, low, norm_high, norm_mid, norm_low = pieces_of(coords, centre)
    one = jnp.ones_like(norm_high)
    empty = jnp.zeros((8, 128), BF16)
    rows = jnp.concatenate([high, high, norm_high, norm_mid, high, mid, norm_low, one, mid, low, one, one], axis=0)
    half = low_lanes(24)
    half_values = low_lanes(RHS)
    scaled = values * SIGNAL
    for pair in range(BZ // 2):
        lanes = slice(pair * 128, pair * 128 + 128)
        tile, tile_values = rows[:, lanes], scaled[:, lanes]
        turned, turned_values = pltpu.roll(tile, LEAF, 1), pltpu.roll(tile_values, LEAF, 1)
        at = col * BZ + 2 * pair
        sources[at] = jnp.concatenate([jnp.where(half, tile, turned).astype(BF16), empty], axis=0)
        sources[at + 1] = jnp.concatenate([jnp.where(half, turned, tile).astype(BF16), empty], axis=0)
        charge[at] = jnp.concatenate(halves(jnp.where(half_values, tile_values, turned_values)), axis=0)
        charge[at + 1] = jnp.concatenate(halves(jnp.where(half_values, turned_values, tile_values)), axis=0)


def build_targets(coords, centre, targets, leaf):
    high, mid, low, norm_high, norm_mid, norm_low = pieces_of(coords, centre)
    one = jnp.ones_like(norm_high)
    rows = jnp.concatenate(
        [
            -2.0 * high, -2.0 * mid, one, one, -2.0 * low, -2.0 * high, one, norm_high,
            -2.0 * mid, -2.0 * high, norm_mid, norm_low, jnp.zeros((8, COL), F32),
        ],
        axis=0,
    )
    for pair in range(BZ // 2):
        tile = rows[:, pair * 128 : pair * 128 + 128].T.astype(BF16)
        targets[leaf + 2 * pair] = tile[:LEAF]
        targets[leaf + 2 * pair + 1] = tile[LEAF:]


def centre_of():
    top, leaf = lax.axis_index("top"), lax.axis_index("leaf")
    row = lax.broadcasted_iota(jnp.int32, (3, COL), 0)
    return jnp.where(row == 0, top.astype(F32) + 0.5, jnp.where(row == 1, leaf.astype(F32) + 0.5, 1.0))


def region(array, columns, first, count, to, centre, sources, charge):
    together = 4 if count % 4 == 0 else 2

    def step(index, carry):
        for part in range(together):
            i = together * index + part
            coords = coords_at(array, columns, first + i, part % 2)
            build_column(coords, array[:, column(first + i)], centre, to(i), sources, charge)
        return carry

    lax.fori_loop(0, count // together, step, 0)


def own_columns(coords, values, to, centre, sources, charge):
    def step(index, carry):
        for part in range(4):
            i = 4 * index + part
            at = column(i)
            build_column(coords[:, at], values[:, at], centre, to(i), sources, charge)
        return carry

    lax.fori_loop(0, COLS // 4, step, 0)


def gathered(array, ids, slot, target):
    half = low_lanes(32)
    four = [array[ids[slot + k, target]] for k in range(4)]
    return jnp.concatenate([jnp.where(half, four[0], four[1]), jnp.where(half, four[2], four[3])], axis=1)


def entries_of(square):
    square = jnp.maximum(square, 1e-20)
    scaled = square * lax.rsqrt(square)
    decay = jnp.exp2(scaled * -LOG2E)
    return jnp.concatenate(halves(decay + scaled * decay), axis=0)


def list_steps(steps, units, choose, ids, sources, charge, targets, squares, add):
    def distances(step, unit):
        target, slot = choose(step, unit)
        squares[unit] = dot(targets[target], gathered(sources, ids, slot, target))

    for unit in range(units):
        distances(0, unit)

    def run(step, carry):
        waiting = None
        for unit in range(units + 1):
            if unit < units:
                entries = entries_of(squares[unit])
                distances(jnp.minimum(step + 1, steps - 1), unit)
            if waiting is not None:
                target, slot = choose(step, unit - 1)
                product = dot(gathered(charge, ids, slot, target), waiting, NT)
                add(step, unit - 1, target, product[:RHS] + product[RHS:])
            waiting = entries
        return carry

    lax.fori_loop(0, steps, run, 0)


def near_pass(phase, cells, table, points, centre, sources, charge, targets, squares, sums):
    for x, y in cells:
        col = x * BY + y
        build_targets(points[:, col * COL : col * COL + COL], centre, targets, col * BZ)

        def zero(i, carry, first=col * BZ):
            sums[first + i] = jnp.zeros((RHS, 128), F32)
            return carry

        lax.fori_loop(0, BZ, zero, 0)
    sources[NEAR_NULL] = jnp.zeros((32, 128), BF16)
    charge[NEAR_NULL] = jnp.zeros((32, 128), BF16)

    def choose(step, unit):
        place = step * UNITS + unit
        code = table[WORK_ROW + 4 * phase + (place >> 7), place & 127]
        return code >> 3, (code & 7) * 4

    def add(step, unit, target, value):
        sums[target] = sums[target] + value

    steps = jnp.maximum((table[COUNT_ROW + phase, 0] + UNITS - 1) // UNITS, 1)
    list_steps(steps, UNITS, choose, table, sources, charge, targets, squares, add)


def folded(sums, pair):
    first, second = sums[2 * pair], sums[2 * pair + 1]
    first = first + pltpu.roll(first, LEAF, 1)
    second = second + pltpu.roll(second, LEAF, 1)
    return jnp.where(low_lanes(RHS), first, second)


def near_store(cells, out, places, sums, charges):
    for (x, y), to in zip(cells, places):
        for pair in range(BZ // 2):
            at = (x * BY + y) * COL + pair * 128
            value = folded(sums, (x * BY + y) * (BZ // 2) + pair)
            out[0:RHS, to * COL + pair * 128 : to * COL + pair * 128 + 128] = value + NUGGET * charges[:, at : at + 128]


def near_own(points, charges, centre, sources, charge):
    own_columns(points, charges, lambda i: (i // BY + 1) * NX + i % BY + 1, centre, sources, charge)


def near_sides(from_down, from_up, centre, sources, charge):
    region(from_down, YCOLS, YFAR, YNEAR, lambda i: (i + 1) * NX, centre, sources, charge)
    region(from_up, YCOLS, YFAR, YNEAR, lambda i: (i + 1) * NX + NX - 1, centre, sources, charge)


def inner_kernel(table, points, charges, out, sources, charge, targets, squares, sums):
    centre = centre_of()
    near_own(points, charges, centre, sources, charge)
    near_pass(0, INNER, table, points, centre, sources, charge, targets, squares, sums)
    near_store(INNER, out, range(4), sums, charges)


def strip_kernel(
    table, points, charges, skeleton, coef, from_down, from_up,
    out, far_sources, far_charge, far_targets, sources, charge,
    targets, squares, sums,
):
    centre = centre_of()
    near_own(points, charges, centre, sources, charge)
    near_sides(from_down, from_up, centre, sources, charge)
    near_pass(1, STRIP, table, points, centre, sources, charge, targets, squares, sums)
    near_store(STRIP, out, range(4), sums, charges)
    own_columns(skeleton, coef, lambda i: i, centre, far_sources, far_charge)
    region(from_down, YCOLS, 0, YFAR, lambda i: COLS + i, centre, far_sources, far_charge)
    region(from_up, YCOLS, 0, YFAR, lambda i: COLS + YFAR + i, centre, far_sources, far_charge)

    def target_step(i, carry):
        for part in range(2):
            col = 2 * i + part
            build_targets(skeleton[:, column(col)], centre, far_targets, col * BZ)
        return carry

    lax.fori_loop(0, COLS // 2, target_step, 0)


def rest_kernel(
    table, points, charges, from_down, from_up, from_left, from_right,
    inner, strip, early_sources, early_charge, far_targets, near_sources, near_charge, out,
    sources, charge, targets, far_sources, far_charge, squares, sums,
):
    centre = centre_of()
    def keep(i, carry):
        for leaf in range(BZ):
            at = NX * BZ + i * BZ + leaf
            sources[at] = near_sources[at]
            charge[at] = near_charge[at]
        return carry

    lax.fori_loop(0, BX * NX, keep, 0)
    region(from_left, XCOLS, XFAR, XNEAR, lambda i: i, centre, sources, charge)
    region(from_right, XCOLS, XFAR, XNEAR, lambda i: (NX - 1) * NX + i, centre, sources, charge)
    near_pass(2, RIM, table, points, centre, sources, charge, targets, squares, sums)
    near_store(RIM, out, [x * BY + y for x, y in RIM], sums, charges)
    for cells, done in ((INNER, inner), (STRIP, strip)):
        for i, (x, y) in enumerate(cells):
            out[0:RHS, column(x * BY + y)] = done[:, i * COL : i * COL + COL]

    def place(first, count, to):
        def step(i, carry):
            for leaf in range(BZ):
                at, source = to(i) * BZ + leaf, (first + i) * BZ + leaf
                far_sources[at] = early_sources[source]
                far_charge[at] = early_charge[source]
            return carry

        lax.fori_loop(0, count, step, 0)

    place(0, COLS, lambda i: (i // BY + 2) * FX + i % BY + 2)
    place(COLS, YFAR, lambda i: (i // 2 + 2) * FX + i % 2)
    place(COLS + YFAR, YFAR, lambda i: (i // 2 + 2) * FX + i % 2 + BY + 2)
    region(from_left, XCOLS, 0, XFAR, lambda i: i, centre, far_sources, far_charge)
    region(from_right, XCOLS, 0, XFAR, lambda i: (BX + 2) * FX + i, centre, far_sources, far_charge)

    def choose(step, unit):
        return step * 16 + unit // 4, FAR_ROW + unit % 4 * 4

    def add(step, unit, target, value):
        sums[target] = value if unit % 4 == 0 else sums[target] + value

    list_steps(HERE * 4 // 64, 64, choose, table, far_sources, far_charge, far_targets, squares, add)

    def far_store(i, carry):
        out[RHS : 2 * RHS, pl.ds(pl.multiple_of(i * 128, 128), 128)] = folded(sums, i)
        return carry

    lax.fori_loop(0, HERE // 2, far_store, 0)


def last_kernel(
    device_far, rows, device_skeleton, branch_skeleton, branch_transfer, transfer, basis, near_far, out, coupling
):
    @pl.when(pl.program_id(0) == 0)
    def start():
        top, leaf = lax.axis_index("top"), lax.axis_index("leaf")
        same = lax.broadcasted_iota(jnp.int32, (LEAF, LEAF), 0) == lax.broadcasted_iota(
            jnp.int32, (LEAF, LEAF), 1
        )

        def upright(coords):
            return [
                jnp.sum(jnp.where(same, coords[i : i + 1], 0.0), axis=1, keepdims=True) for i in range(3)
            ]

        def kernel_block(own, other):
            total = 0.0
            for i in range(3):
                differ = own[i] - other[i : i + 1]
                total = total + differ * differ
            scaled = KERNEL_SCALE * jnp.sqrt(total)
            return SIGNAL * (1.0 + scaled) * jnp.exp(-scaled)

        def exact(a, b, dims):
            return lax.dot_general(a, b, dims, precision=EXACT, preferred_element_type=F32)

        def cluster(skeletons, index):
            tile = skeletons[:, pl.ds(pl.multiple_of(index // 2 * 128, 128), 128)]
            return jnp.where(index % 2 == 0, tile, pltpu.roll(tile, LEAF, 1))[:, :LEAF]

        own = upright(cluster(device_skeleton, top * 16 + leaf))
        coupled = jnp.zeros((RHS, LEAF), F32)
        for k in range(4):
            partner = jnp.minimum(jnp.maximum(device_far[k, 0], 0), 127)
            coupled = coupled + exact(rows[partner][:, :LEAF], kernel_block(own, cluster(device_skeleton, partner)), NT)
        own = upright(cluster(branch_skeleton, top))
        field = jnp.zeros((RHS, LEAF), F32)
        for e in range(8):
            total = rows[16 * e]
            for d in range(1, 16):
                total = total + rows[16 * e + d]
            weight = jnp.where(jnp.abs(e - top) >= 2, 1.0, 0.0)
            field = field + exact(total[:, LEAF:] * weight, kernel_block(own, cluster(branch_skeleton, e)), NT)
        coupled = coupled + exact(field, branch_transfer[...], NN)
        coupling[...] = coupled

    lifted = jnp.concatenate(halves(coupling[...]), axis=0)
    half = low_lanes(RHS)
    together = BLOCK // 256

    places, fields = [], []
    for part in range(together):
        place = slice(part * 256, part * 256 + 256)
        t_high, t_low = halves(transfer[:, place])
        up = dot(lifted, t_high) + dot(lifted, t_low)
        places.append(place)
        fields.append(near_far[RHS : 2 * RHS, place] + (up[:RHS] + up[RHS:]))
    products = []
    for place, value in zip(places, fields):
        pieces = []
        for i in range(4):
            tile = value[:, (i // 2) * 128 : (i // 2) * 128 + 128]
            tile = jnp.where(half, tile, 0.0) if i % 2 == 0 else jnp.where(half, 0.0, tile)
            pieces.extend(halves(tile))
        lines = jnp.concatenate(pieces, axis=0)
        b_high, b_low = halves(basis[:, place])
        products.append(
            dot(lines, jnp.concatenate([b_high, b_high], axis=0))
            + dot(lines, jnp.concatenate([b_low, b_low], axis=0))
        )
    for place, product in zip(places, products):
        each = [product[32 * i : 32 * i + 16] + product[32 * i + 16 : 32 * i + 32] for i in range(4)]
        result = jnp.concatenate(
            [
                jnp.where(half, each[0][:, :128], each[1][:, :128]),
                jnp.where(half, each[2][:, 128:], each[3][:, 128:]),
            ],
            axis=1,
        )
        out[:, place] = near_far[0:RHS, place] + result


def block(rows):
    return pl.BlockSpec((rows, BLOCK), lambda i: (0, i))


def shape(*dims, dtype=F32):
    return jax.ShapeDtypeStruct(dims, dtype)


def body(
    points,
    charges,
    near_list,
    far_list,
    leaf_basis,
    transfer,
    leaf_skeleton,
    device_far,
    branch_transfer,
    device_skeleton,
    branch_skeleton,
):
    here = charges.shape[1]

    def moved(array, axis, up):
        size = lax.axis_size(axis)
        pairs = [(i, i + 1) for i in range(size - 1)]
        return lax.ppermute(array, axis, pairs if up else [(j, i) for i, j in pairs])

    coef, device_row, table, send_down, send_up = pl.pallas_call(
        first_kernel,
        grid=(here // BLOCK,),
        in_specs=[VMEM] * 4 + [block(RANK)] * 2 + [VMEM] * 2,
        out_specs=[VMEM] * 5,
        scratch_shapes=[pltpu.VMEM((2 * RHS, LEAF), F32)],
        out_shape=[
            shape(RHS, here), shape(RHS, 128), shape(64, HERE, dtype=jnp.int32), shape(RHS, YLANES), shape(RHS, YLANES),
        ],
        compiler_params=room(60),
        name="coefficients",
    )(points, charges, near_list, far_list, leaf_basis, transfer, leaf_skeleton, branch_transfer)
    every_row = lax.all_gather(device_row, ("top", "leaf"), axis=0)
    from_down = moved(send_up, "leaf", True)
    from_up = moved(send_down, "leaf", False)

    def scratch(leaves):
        return [
            pltpu.VMEM((leaves, 32, 128), BF16),
            pltpu.VMEM((leaves, 32, 128), BF16),
            pltpu.VMEM((HERE, LEAF, 32), BF16),
        ]

    common = [pltpu.VMEM((64, LEAF, 4 * LEAF), F32), pltpu.VMEM((HERE, RHS, 128), F32)]

    def cost(us):
        return pl.CostEstimate(flops=us * 10**9, bytes_accessed=10**6, transcendentals=0)

    inner = pl.pallas_call(
        inner_kernel,
        in_specs=[SMEM] + [VMEM] * 2,
        out_specs=VMEM,
        out_shape=shape(RHS, 4 * COL),
        scratch_shapes=scratch(NEAR_NULL + 1) + common,
        compiler_params=room(16),
        cost_estimate=cost(13),
        name="inner",
    )(table, points, charges)
    send_left, send_right = pl.pallas_call(
        side_kernel,
        in_specs=[VMEM] * 6,
        out_specs=[VMEM] * 2,
        out_shape=[shape(RHS, XLANES), shape(RHS, XLANES)],
        compiler_params=room(12),
        name="sides",
    )(points, charges, leaf_skeleton, coef, from_down, from_up)
    from_left = moved(send_right, "top", True)
    from_right = moved(send_left, "top", False)
    early = (COLS + 2 * YFAR) * BZ
    strip, early_sources, early_charge, far_targets, near_sources, near_charge = pl.pallas_call(
        strip_kernel,
        in_specs=[SMEM] + [VMEM] * 6,
        out_specs=[VMEM] * 6,
        out_shape=[
            shape(RHS, 4 * COL), shape(early, 32, 128, dtype=BF16), shape(early, 32, 128, dtype=BF16),
            shape(HERE, LEAF, 32, dtype=BF16), shape(NEAR_NULL + 1, 32, 128, dtype=BF16),
            shape(NEAR_NULL + 1, 32, 128, dtype=BF16),
        ],
        scratch_shapes=scratch(NEAR_NULL + 1)[2:] + common,
        compiler_params=room(28),
        cost_estimate=cost(15),
        name="strip",
    )(table, points, charges, leaf_skeleton, coef, from_down, from_up)
    near_far = pl.pallas_call(
        rest_kernel,
        in_specs=[SMEM] + [VMEM] * 13,
        out_specs=VMEM,
        out_shape=shape(2 * RHS, here),
        scratch_shapes=scratch(NEAR_NULL + 1) + scratch(FAR_ALL)[:2] + common,
        compiler_params=room(38),
        cost_estimate=cost(55),
        name="rest",
    )(
        table, points, charges, from_down, from_up, from_left, from_right,
        inner, strip, early_sources, early_charge, far_targets, near_sources, near_charge,
    )
    return pl.pallas_call(
        last_kernel,
        grid=(here // BLOCK,),
        in_specs=[SMEM] + [VMEM] * 4 + [block(RANK)] * 2 + [block(2 * RHS)],
        out_specs=block(RHS),
        scratch_shapes=[pltpu.VMEM((RHS, LEAF), F32)],
        out_shape=shape(RHS, here),
        compiler_params=room(60),
        name="fields",
    )(
        device_far,
        every_row,
        device_skeleton,
        branch_skeleton,
        branch_transfer,
        transfer,
        leaf_basis,
        near_far,
    )


def solution(mesh):
    split = P(None, ("top", "leaf"))
    return jax.shard_map(
        body, mesh=mesh, in_specs=(split,) * 9 + (P(), P()), out_specs=split, check_vma=False
    )
```
